32 devices in a mesh: dp: 8 (over y, x, core), tensor: 4 (over z).
Axes of the slice: x: 2, y: 2, z: 4, core: 2. Of those that a mesh axis runs over, the one named last changes fastest.
Arguments:
- output_gradient: bfloat16 [2048, 8192], P('dp', 'tensor'), may hold values from -96 to 96
- hidden: bfloat16 [2048, 28672], P('dp', 'tensor'), may hold values from -3 to 3
- adapter_down: bfloat16 [16, 16, 28672], P('dp', None, 'tensor'), may hold values from -0.03125 to 0.03125
- adapter_up: bfloat16 [16, 16, 8192], P('dp', None, 'tensor'), may hold values from -0.0625 to 0.0625
- counts: int32 [16], replicated, may hold values from 32 to 288, as said below
- offsets: int32 [16], replicated, may hold values from 0 to 2016, as said below
- adapter_slot: int32 [16], replicated, may hold values from 0 to 15, as said below
Outputs:
- adapter_hidden_gradient: bfloat16 [2048, 28672], P('dp', 'tensor')
- adapter_down_gradient: float32 [16, 16, 28672], P('dp', None, 'tensor')
- adapter_up_gradient: float32 [16, 16, 8192], P('dp', None, 'tensor')
The draws below stay inside these ranges and needn't reach their ends.
Inputs may be any that keep to these rules, and one draw needn't show every extreme that they name: counts sum to 2048; the last adapter has exactly 32 tokens; exactly one adapter has 288 tokens, every other fewer. Tokens are grouped by adapter in increasing order: offsets[a] is the sum of counts of the adapters before a. `adapter_slot`: every slot holds exactly one adapter; slot k lies on dp index k // 2, and any 16 // 2 adapters in a row lie on distinct dp indices.
All inputs are finite; a program needn't handle non-finite values.
Results may differ from the reference program's by a relative error of at most 0.0075.
Values may be sent and summed in bfloat16 or wider, within the bound.
A program may use at most 64 MiB of HBM per device.

```python
import math
import jax
import jax.numpy as jnp
import numpy as np
from jax import lax

MODEL_DIM = 8192
HIDDEN_DIM = 28672
ADAPTER_RANK = 16
TOK_DEV = 256
ADP_DEV = 2
MIN_COUNT = 32
MIXTURE_ADAPTERS = 16
TOKENS = 2048


def layout_tables():
    devices = TOKENS // TOK_DEV
    dense_count = TOK_DEV // MIN_COUNT
    long_units = min(4, (devices - 2) // 3)
    drawn_units = devices - 2 - 3 * long_units
    piece_floor = []
    piece_base = []
    piece_head = []
    piece_tail = []
    for long_index in range(long_units):
        piece_floor.append(TOK_DEV - 12)
        piece_base.append(TOK_DEV)
        piece_head.append(long_index)
        piece_tail.append(-1)
        piece_floor.append(TOK_DEV - MIN_COUNT + 4)
        piece_base.append(TOK_DEV)
        piece_head.append(-1)
        piece_tail.append(long_index)
    for drawn_index in range(drawn_units):
        piece_floor.append(TOK_DEV)
        piece_base.append(TOK_DEV)
        piece_head.append(-1)
        piece_tail.append(-1)
    piece_floor.append(TOK_DEV - MIN_COUNT)
    piece_base.append(TOK_DEV - MIN_COUNT)
    piece_head.append(-1)
    piece_tail.append(-1)
    piece_number = len(piece_floor)
    final_piece = piece_number - 1
    needed = MIXTURE_ADAPTERS - dense_count - long_units - 1
    per_piece = [1] * piece_number
    spare_slots = needed - piece_number
    visit_order = list(range(2 * long_units, final_piece)) + list(range(2 * long_units)) + [final_piece]
    moved = True
    while spare_slots > 0 and moved:
        moved = False
        for piece_index in visit_order:
            if spare_slots > 0 and per_piece[piece_index] < piece_floor[piece_index] // MIN_COUNT:
                per_piece[piece_index] += 1
                spare_slots -= 1
                moved = True
    unit_of = []
    within_unit = []
    kind_of = []
    piece_of = []
    rank_of = []
    long_of = []

    def append_row(unit_number, within_number, kind_number, piece_number_row, rank_number, long_number):
        unit_of.append(unit_number)
        within_unit.append(within_number)
        kind_of.append(kind_number)
        piece_of.append(piece_number_row)
        rank_of.append(rank_number)
        long_of.append(long_number)
    for dense_index in range(dense_count):
        append_row(0, dense_index, 0, 0, 0, 0)
    for long_index in range(long_units):
        unit_number = 1 + long_index
        within_number = 0
        for rank_number in range(per_piece[2 * long_index]):
            append_row(unit_number, within_number, 2, 2 * long_index, rank_number, 0)
            within_number += 1
        append_row(unit_number, within_number, 1, 0, 0, long_index)
        within_number += 1
        for rank_number in range(per_piece[2 * long_index + 1]):
            append_row(unit_number, within_number, 2, 2 * long_index + 1, rank_number, 0)
            within_number += 1
    for drawn_index in range(drawn_units):
        unit_number = 1 + long_units + drawn_index
        piece_index = 2 * long_units + drawn_index
        for rank_number in range(per_piece[piece_index]):
            append_row(unit_number, rank_number, 2, piece_index, rank_number, 0)
    unit_number = 1 + long_units + drawn_units
    for rank_number in range(per_piece[final_piece]):
        append_row(unit_number, rank_number, 2, final_piece, rank_number, 0)
    append_row(unit_number, per_piece[final_piece], 0, 0, 0, 0)
    unit_total = unit_number + 1
    return (np.array(unit_of, np.int32), np.array(within_unit, np.int32), np.array(kind_of, np.int32), np.array(piece_of, np.int32), np.array(rank_of, np.int32), np.array(long_of, np.int32), np.array(per_piece, np.int32), np.array(piece_base, np.int32), np.array(piece_head, np.int32), np.array(piece_tail, np.int32), long_units, unit_total)


def split_counts(key):
    tables = layout_tables()
    unit_of, within_unit, kind_of, piece_of, rank_of, long_of = tables[0:6]
    per_piece, piece_base, piece_head, piece_tail, long_units, unit_total = tables[6:12]
    piece_number = piece_base.shape[0]
    base_key = jax.random.fold_in(key, 7)
    big_key, small_key, tail_key, weight_key, shuffle_key = jax.random.split(base_key, 5)
    long_ids = jnp.arange(long_units, dtype=jnp.int32)
    is_big = long_ids == 0
    head_big = jax.random.randint(big_key, (long_units,), 4, 13)
    head_small = jax.random.randint(small_key, (long_units,), 4, 12)
    head_cut = jnp.where(is_big, head_big, head_small)
    tail_low = MIN_COUNT - 12
    tail_span = jnp.maximum(MIN_COUNT - tail_low - head_cut, 1)
    tail_small = tail_low + jax.random.randint(tail_key, (long_units,), 0, tail_span)
    tail_cut = jnp.where(is_big, MIN_COUNT - head_cut, tail_small)
    long_count = TOK_DEV + head_cut + tail_cut
    head_index = jnp.asarray(np.maximum(piece_head, 0))
    tail_index = jnp.asarray(np.maximum(piece_tail, 0))
    head_mask = jnp.asarray(piece_head >= 0)
    tail_mask = jnp.asarray(piece_tail >= 0)
    piece_length = jnp.asarray(piece_base) - jnp.where(head_mask, head_cut[head_index], 0) - jnp.where(tail_mask, tail_cut[tail_index], 0)
    members = ((kind_of == 2)[:, None] & (piece_of[:, None] == np.arange(piece_number)[None, :])).astype(np.int32)
    member_int = jnp.asarray(members)
    filler_mask = jnp.asarray(kind_of == 2)
    piece_ids = jnp.asarray(piece_of)
    weights = jax.random.randint(weight_key, (MIXTURE_ADAPTERS,), 1, 4)
    weight_total = jnp.sum(member_int * weights[:, None], axis=0)
    spare_tokens = piece_length - jnp.asarray(per_piece) * MIN_COUNT
    own_spare = spare_tokens[piece_ids]
    own_total = jnp.maximum(weight_total[piece_ids], 1)
    extras = jnp.where(filler_mask, own_spare * weights // own_total, 0)
    leftover = spare_tokens - jnp.sum(member_int * extras[:, None], axis=0)
    extras = extras + jnp.where(filler_mask & (jnp.asarray(rank_of) < leftover[piece_ids]), 1, 0)
    canonical = jnp.where(jnp.asarray(kind_of == 1), long_count[jnp.asarray(long_of)], jnp.where(filler_mask, MIN_COUNT + extras, MIN_COUNT))
    unit_position = jnp.concatenate([jax.random.permutation(shuffle_key, unit_total - 1).astype(jnp.int32), jnp.array([unit_total - 1], jnp.int32)])
    sort_key = unit_position[jnp.asarray(unit_of)] * MIXTURE_ADAPTERS + jnp.asarray(within_unit)
    ordering = jnp.argsort(sort_key, stable=True)
    return canonical[ordering].astype(jnp.int32)


def draw_counts(key, part):
    return split_counts(key)


def draw_offsets(key, part):
    sizes_drawn = split_counts(key)
    return (jnp.cumsum(sizes_drawn) - sizes_drawn).astype(jnp.int32)


def draw_adapter_slot(key, part):
    base_key = jax.random.fold_in(key, 11)
    shift_key, turn_key = jax.random.split(base_key, 2)
    owners = MIXTURE_ADAPTERS // ADP_DEV
    indices = jnp.arange(MIXTURE_ADAPTERS, dtype=jnp.int32)
    shift_value = jax.random.randint(shift_key, (), 0, owners)
    turns = jax.random.randint(turn_key, (owners,), 0, ADP_DEV)
    device_of = (indices + shift_value) % owners
    within = (indices // owners + turns[device_of]) % ADP_DEV
    return (device_of * ADP_DEV + within).astype(jnp.int32)


def block_levels(rng, dims, cuts, low, top_value):
    def one(axis_at, shards_of):
        heights = jax.random.uniform(jax.random.fold_in(jax.random.fold_in(rng, 6), axis_at), (shards_of,), jnp.float32, low / len(cuts), top_value / len(cuts))
        return jnp.repeat(jnp.exp(heights), dims[axis_at] // shards_of).reshape((-1,) + (1,) * (len(dims) - axis_at - 1))

    level = one(*cuts[0])
    for cut in cuts[1:]:
        level = level * one(*cut)
    return level


def noise(stream_key, extent, scale, limit, pieces=(), kind=jnp.bfloat16):
    entries = scale * jax.random.normal(stream_key, extent, jnp.float32)
    if pieces:
        entries = entries * block_levels(stream_key, extent, pieces, -0.22, 0.18)
    return jnp.clip(entries, -limit, limit).astype(kind)


def setup_inputs(seed: int = 0) -> dict:
    seeds = jax.random.split(jax.random.key(seed), 8)
    output_gradient = noise(seeds[0], (TOKENS, MODEL_DIM), 16.0, 96.0, ((0, 8), (1, 4)))
    hidden = noise(seeds[1], (TOKENS, HIDDEN_DIM), 0.5, 3.0, ((0, 8), (1, 4)))
    adapter_down = noise(seeds[2], (MIXTURE_ADAPTERS, ADAPTER_RANK, HIDDEN_DIM), HIDDEN_DIM ** -0.5, 0.03125, ((0, 8), (2, 4)))
    adapter_up = noise(seeds[3], (MIXTURE_ADAPTERS, ADAPTER_RANK, MODEL_DIM), MODEL_DIM ** -0.5, 0.0625, ((0, 8), (2, 4)))
    counts = draw_counts(jax.random.fold_in(seeds[7], 71), 0)
    offsets = draw_offsets(jax.random.fold_in(seeds[7], 71), 0)
    adapter_slot = draw_adapter_slot(jax.random.fold_in(seeds[7], 71), 0)
    return dict(output_gradient=output_gradient, hidden=hidden, adapter_down=adapter_down, adapter_up=adapter_up, counts=counts, offsets=offsets, adapter_slot=adapter_slot)


adapter_factor = 2.0


def reference(output_gradient, hidden, adapter_down, adapter_up, counts, offsets, adapter_slot):
    token_count = output_gradient.shape[0]
    adapter_list = adapter_down.shape[0]
    adapter_rank = adapter_down.shape[1]
    hidden_size_count = hidden.shape[1]
    model_feature_width = output_gradient.shape[1]
    rows_per_block = math.gcd(token_count, 1024)
    block_total = token_count // rows_per_block
    down_flattened = adapter_down.reshape(adapter_list * adapter_rank, hidden_size_count)
    up_flattened = adapter_up.reshape(adapter_list * adapter_rank, model_feature_width)
    columns = lax.broadcasted_iota(jnp.int32, (1, adapter_list), 1)
    segment_ends = offsets + counts

    def pick(value_entries, flattened_rows, member_rows_float):
        rank_scores = lax.dot_general(value_entries, flattened_rows, (((1,), (1,)), ((), ())), preferred_element_type=jnp.float32)
        return jnp.sum(rank_scores.reshape(value_entries.shape[0], adapter_list, adapter_rank) * member_rows_float[:, :, None], axis=1)

    def run_block(carry_pair, block_index):
        down_running, up_running = carry_pair
        first_row = block_index * rows_per_block
        grad_block = lax.dynamic_slice_in_dim(output_gradient, first_row, rows_per_block, 0)
        hidden_block = lax.dynamic_slice_in_dim(hidden, first_row, rows_per_block, 0)
        positions = first_row + lax.broadcasted_iota(jnp.int32, (rows_per_block, 1), 0)
        inside = (positions >= offsets[None, :]) & (positions < segment_ends[None, :])
        slot_of_row = jnp.sum(jnp.where(inside, adapter_slot[None, :], 0), axis=1)
        member_rows = (slot_of_row[:, None] == columns).astype(jnp.bfloat16)
        member_rows_float = member_rows.astype(jnp.float32)
        up_incoming = pick(grad_block, up_flattened, member_rows_float).astype(jnp.bfloat16)
        down_incoming = pick(hidden_block, down_flattened, member_rows_float).astype(jnp.bfloat16)
        broadcast_up = (member_rows[:, :, None] * up_incoming[:, None, :]).reshape(rows_per_block, adapter_list * adapter_rank)
        broadcast_down = (member_rows[:, :, None] * down_incoming[:, None, :]).reshape(rows_per_block, adapter_list * adapter_rank)
        hidden_gradient = jnp.dot(broadcast_up, down_flattened, preferred_element_type=jnp.float32)
        hidden_gradient = (adapter_factor * hidden_gradient).astype(jnp.bfloat16)
        down_running = down_running + lax.dot_general(broadcast_up, hidden_block, (((0,), (0,)), ((), ())), preferred_element_type=jnp.float32)
        up_running = up_running + lax.dot_general(broadcast_down, grad_block, (((0,), (0,)), ((), ())), preferred_element_type=jnp.float32)
        return (down_running, up_running), hidden_gradient

    initial_pair = (jnp.zeros((adapter_list * adapter_rank, hidden_size_count), jnp.float32),
                  jnp.zeros((adapter_list * adapter_rank, model_feature_width), jnp.float32))
    (down_running, up_running), grad_blocks = lax.scan(run_block, initial_pair, jnp.arange(block_total, dtype=jnp.int32))
    adapter_hidden_gradient = grad_blocks.reshape(token_count, hidden_size_count)
    slot_grid = adapter_slot[:, None] == columns
    total_slots = jnp.sum(jnp.where(slot_grid, counts[:, None], 0), axis=0)
    scale_entries = adapter_factor / total_slots.astype(jnp.float32)
    adapter_down_gradient = down_running.reshape(adapter_list, adapter_rank, hidden_size_count) * scale_entries[:, None, None]
    adapter_up_gradient = up_running.reshape(adapter_list, adapter_rank, model_feature_width) * scale_entries[:, None, None]
    return adapter_hidden_gradient, adapter_down_gradient, adapter_up_gradient
```

```python
import functools
import math

import jax
import jax.numpy as jnp
from jax import lax
from jax.experimental import pallas as pl
from jax.experimental.pallas import tpu as pltpu
from jax.sharding import PartitionSpec as P

adapter_factor = 2.0
MESH = pl.DeviceIdType.MESH


def chip_grid(dp_count):
    chips = dp_count // 2
    second = max(d for d in range(1, math.isqrt(chips) + 1) if chips % d == 0)
    return chips // second, second


def kernel(
    dp_count, tensor_count, sends,
    counts, offsets, slots, og, hid, adn, aup,
    out_h, out_d, out_u,
    gath_d, gath_u, z_up, z_dn,
    sib_d, sib_u, got_d, got_u, sum_d, sum_u,
    one_d0, one_d1, one_u0, one_u1, two_d0, two_d1, two_u0, two_u1,
    send_sem, gath_sem, z_sem, sib_sem, one_sem0, one_sem1, two_sem0, two_sem1,
):
    size_a, size_b = chip_grid(dp_count)
    chips = size_a * size_b
    tokens = og.shape[0]
    per_owner, rank = adn.shape[0], adn.shape[1]
    me = lax.axis_index("dp")
    me_t = lax.axis_index("tensor")
    core = me % 2
    chip = me // 2
    at_a, at_b = chip // size_b, chip % size_b
    sibling = chip * 2 + (1 - core)

    def chip_of(half, first, second):
        return first * size_b + second if half == 0 else second * size_b + first

    def axes(half):
        if half == 0:
            return at_a, size_a, at_b, size_b
        return at_b, size_b, at_a, size_a

    started = []

    def push(src, dst, recv, **device):
        copy = pltpu.make_async_remote_copy(
            src_ref=src, dst_ref=dst, send_sem=send_sem.at[len(started)], recv_sem=recv,
            device_id=device, device_id_type=MESH,
        )
        copy.start()
        started.append(copy)

    def arrived(dst, recv):
        pltpu.make_async_remote_copy(
            src_ref=dst, dst_ref=dst, send_sem=send_sem.at[0], recv_sem=recv,
            device_id={"dp": sibling}, device_id_type=MESH,
        ).wait_recv()

    barrier = pltpu.get_barrier_semaphore()
    partners = [{"dp": sibling}]
    for off in range(1, size_a):
        partners.append({"dp": (((at_a + off) % size_a) * size_b + at_b) * 2 + core})
    for off in range(1, size_b):
        partners.append({"dp": (at_a * size_b + (at_b + off) % size_b) * 2 + core})
    for off in range(1, tensor_count):
        partners.append({"tensor": (me_t + off) % tensor_count})
    for partner in partners:
        pl.semaphore_signal(barrier, inc=1, device_id=partner, device_id_type=MESH)
    pl.semaphore_wait(barrier, len(partners))

    def gather_own(which, own, gath):
        for half in range(per_owner):
            first, n_first, second, n_second = axes(half)
            recv = gath_sem.at[which, me, half]
            for off in range(1, n_first):
                to = chip_of(half, (first + off) % n_first, second) * 2 + core
                push(own.at[half], gath.at[me, half], recv, dp=to)
            for off in range(1, n_second):
                to = chip_of(half, first, (second + off) % n_second) * 2 + core
                push(own.at[half], gath.at[me, half], recv, dp=to)
            push(own.at[half], gath.at[me, half], recv, dp=sibling)

    def gather_first(which, gath):
        for half in range(per_owner):
            first, n_first, second, n_second = axes(half)
            for off in range(1, n_first):
                origin = chip_of(half, (first + off) % n_first, second) * 2 + core
                block, recv = gath.at[origin, half], gath_sem.at[which, origin, half]
                arrived(block, recv)
                for off2 in range(1, n_second):
                    to = chip_of(half, first, (second + off2) % n_second) * 2 + core
                    push(block, block, recv, dp=to)
                push(block, block, recv, dp=sibling)

    def gather_second(which, gath):
        for near in (True, False):
            for half in range(per_owner):
                first, n_first, second, n_second = axes(half)
                for off2 in range(1, n_second):
                    for off in range(0, 1) if near else range(1, n_first):
                        origin = chip_of(
                            half, (first + off) % n_first, (second + off2) % n_second
                        ) * 2 + core
                        block, recv = gath.at[origin, half], gath_sem.at[which, origin, half]
                        arrived(block, recv)
                        push(block, block, recv, dp=sibling)

    def gather_sibling(which, gath):
        for other in range(chips):
            for half in range(per_owner):
                origin = other * 2 + (1 - core)
                arrived(gath.at[origin, half], gath_sem.at[which, origin, half])

    gather_own(0, aup, gath_u)
    gather_own(1, adn, gath_d)
    gath_u[pl.ds(me, 1)] = aup[...][None]
    gath_d[pl.ds(me, 1)] = adn[...][None]

    position = me * tokens + lax.broadcasted_iota(jnp.int32, (1, tokens), 1)
    slot_of = jnp.zeros((1, tokens), jnp.int32)
    for adapter in range(counts.shape[0]):
        low = offsets[adapter]
        inside = (position >= low) & (position < low + counts[adapter])
        slot_of = slot_of + jnp.where(inside, slots[adapter], 0)

    def tile_of(width):
        return math.gcd(width, 512)

    def partial_signal(values, gath):
        width = values.shape[1]
        tile = tile_of(width)
        rows = dp_count * per_owner * rank

        def step(at, total):
            cols = pl.ds(pl.multiple_of(at * tile, tile), tile)
            maps = gath[:, :, :, cols].reshape(rows, tile)
            return total + lax.dot_general(
                maps, values[:, cols], (((1,), (1,)), ((), ())),
                preferred_element_type=jnp.float32,
            )

        scores = lax.fori_loop(
            0, width // tile, step, jnp.zeros((rows, tokens), jnp.float32)
        ).reshape(dp_count * per_owner, rank, tokens)
        total = jnp.zeros((rank, tokens), jnp.float32)
        for slot in range(dp_count * per_owner):
            total = total + jnp.where(slot_of == slot, scores[slot], 0.0)
        return total

    def share(which, buffer, value):
        buffer[pl.ds(me_t, 1)] = value[None]
        for off in range(1, tensor_count):
            push(
                buffer.at[me_t], buffer.at[me_t], z_sem.at[which, me_t],
                tensor=(me_t + off) % tensor_count,
            )

    def shared(which, buffer):
        for off in range(1, tensor_count):
            origin = (me_t + off) % tensor_count
            arrived(buffer.at[origin], z_sem.at[which, origin])
        total = buffer[0]
        for origin in range(1, tensor_count):
            total = total + buffer[origin]
        return total.astype(jnp.bfloat16).astype(jnp.float32)

    def spread(signal, numbers):
        return jnp.concatenate(
            [jnp.where(slot_of == number, signal, 0.0) for number in numbers], axis=0
        )

    def numbers_of(which_core):
        return [
            (other * 2 + which_core) * per_owner + half
            for other in range(chips)
            for half in range(per_owner)
        ]

    def sums_sibling(which, signal, values, sib, got):
        rows = spread(signal, numbers_of(1 - core)).astype(jnp.bfloat16)
        width = values.shape[1]
        tile = tile_of(width)

        def step(at, _):
            cols = pl.ds(pl.multiple_of(at * tile, tile), tile)
            term = jnp.dot(rows, values[:, cols], preferred_element_type=jnp.float32)
            sib[:, :, :, cols] = term.astype(jnp.bfloat16).reshape(chips, per_owner, rank, tile)
            return 0

        lax.fori_loop(0, width // tile, step, 0)
        push(sib, got, sib_sem.at[which], dp=sibling)

    def sums_first(which, signal, values, got, total, one):
        rows = spread(signal, numbers_of(core)).astype(jnp.bfloat16)
        width = values.shape[1]
        tile = tile_of(width)
        arrived(got, sib_sem.at[which])

        def step(at, _):
            cols = pl.ds(pl.multiple_of(at * tile, tile), tile)
            term = jnp.dot(rows, values[:, cols], preferred_element_type=jnp.float32)
            term = term.reshape(chips, per_owner, rank, tile)
            term = term + got[:, :, :, cols].astype(jnp.float32)
            total[:, :, :, cols] = term.astype(jnp.bfloat16)
            return 0

        lax.fori_loop(0, width // tile, step, 0)
        sems = (one_sem0, one_sem1)
        for far in (True, False):
            for half in range(per_owner):
                first, n_first, second, n_second = axes(half)
                for off in range(1, n_first):
                    peer = (first + off) % n_first
                    to = chip_of(half, peer, second) * 2 + core
                    for off2 in range(1, n_second) if far else range(0, 1):
                        owner_second = (second + off2) % n_second
                        push(
                            total.at[chip_of(half, peer, owner_second), half],
                            one[half].at[first, owner_second],
                            sems[half].at[which, first, owner_second],
                            dp=to,
                        )

    def sums_second(which, total, one, two):
        sems, sems2 = (one_sem0, one_sem1), (two_sem0, two_sem1)
        for half in range(per_owner):
            first, n_first, second, n_second = axes(half)
            for off2 in range(1, n_second):
                owner_second = (second + off2) % n_second
                owner = chip_of(half, first, owner_second)
                value = total[owner, half].astype(jnp.float32)
                for off in range(1, n_first):
                    peer = (first + off) % n_first
                    arrived(
                        one[half].at[peer, owner_second],
                        sems[half].at[which, peer, owner_second],
                    )
                    value = value + one[half][peer, owner_second].astype(jnp.float32)
                total[pl.ds(owner, 1), half] = value.astype(jnp.bfloat16)[None]
                push(
                    total.at[owner, half], two[half].at[second],
                    sems2[half].at[which, second], dp=owner * 2 + core,
                )

    def sums_last(which, total, one, two, out):
        sems, sems2 = (one_sem0, one_sem1), (two_sem0, two_sem1)
        for half in range(per_owner):
            first, n_first, second, n_second = axes(half)
            value = total[chip, half].astype(jnp.float32)
            for off in range(1, n_first):
                peer = (first + off) % n_first
                arrived(one[half].at[peer, second], sems[half].at[which, peer, second])
                value = value + one[half][peer, second].astype(jnp.float32)
            for off2 in range(1, n_second):
                peer = (second + off2) % n_second
                arrived(two[half].at[peer], sems2[half].at[which, peer])
                value = value + two[half][peer].astype(jnp.float32)
            number = me * per_owner + half
            held = jnp.zeros((1, 1), jnp.int32)
            for adapter in range(counts.shape[0]):
                mine = jnp.full((1, 1), slots[adapter], jnp.int32) == number
                held = held + jnp.where(mine, counts[adapter], 0)
            out[half] = value * (adapter_factor / held.astype(jnp.float32))

    one_d, one_u = (one_d0, one_d1), (one_u0, one_u1)
    two_d, two_u = (two_d0, two_d1), (two_u0, two_u1)

    gather_first(0, gath_u)
    gather_second(0, gath_u)
    gather_sibling(0, gath_u)
    share(0, z_up, partial_signal(og, gath_u))
    gather_first(1, gath_d)
    up_signal = shared(0, z_up)
    sums_sibling(0, up_signal, hid, sib_d, got_d)
    gather_second(1, gath_d)
    sums_first(0, up_signal, hid, got_d, sum_d, one_d)
    gather_sibling(1, gath_d)
    share(1, z_dn, partial_signal(hid, gath_d))

    all_rows = dp_count * per_owner * rank
    tokens_by_row = spread(up_signal, range(dp_count * per_owner)).T.astype(jnp.bfloat16)
    tile = tile_of(hid.shape[1])

    def hidden_step(at, _):
        cols = pl.ds(pl.multiple_of(at * tile, tile), tile)
        maps = gath_d[:, :, :, cols].reshape(all_rows, tile)
        term = jnp.dot(tokens_by_row, maps, preferred_element_type=jnp.float32)
        out_h[:, cols] = (adapter_factor * term).astype(out_h.dtype)
        return 0

    lax.fori_loop(0, hid.shape[1] // tile, hidden_step, 0)

    down_signal = shared(1, z_dn)
    sums_sibling(1, down_signal, og, sib_u, got_u)
    sums_second(0, sum_d, one_d, two_d)
    sums_first(1, down_signal, og, got_u, sum_u, one_u)
    sums_second(1, sum_u, one_u, two_u)
    sums_last(0, sum_d, one_d, two_d, out_d)
    sums_last(1, sum_u, one_u, two_u, out_u)
    for copy in started:
        copy.wait_send()
    assert len(started) == sends, (len(started), sends)


def send_count(dp_count, tensor_count, per_owner):
    size_a, size_b = chip_grid(dp_count)
    total = 2 * (tensor_count - 1) + 2
    for half in range(per_owner):
        n_first, n_second = (size_a, size_b) if half == 0 else (size_b, size_a)
        own = n_first + n_second - 1
        relayed = (n_first - 1) * n_second + (n_second - 1) * n_first
        back = (n_first - 1) * n_second + (n_second - 1)
        total += 2 * (own + relayed + back)
    return total


def on_device(output_gradient, hidden, adapter_down, adapter_up, counts, offsets, adapter_slot):
    dp_count, tensor_count = lax.axis_size("dp"), lax.axis_size("tensor")
    size_a, size_b = chip_grid(dp_count)
    chips = size_a * size_b
    per_owner, rank, wide = adapter_down.shape
    narrow = adapter_up.shape[2]
    tokens = hidden.shape[0]
    sends = send_count(dp_count, tensor_count, per_owner)
    bf16, f32 = jnp.bfloat16, jnp.float32
    dma = pltpu.SemaphoreType.DMA
    vmem = pl.BlockSpec(memory_space=pltpu.VMEM)
    smem = pl.BlockSpec(memory_space=pltpu.SMEM)
    scratch = [
        pltpu.VMEM((dp_count, per_owner, rank, wide), bf16),
        pltpu.VMEM((dp_count, per_owner, rank, narrow), bf16),
        pltpu.VMEM((tensor_count, rank, tokens), f32),
        pltpu.VMEM((tensor_count, rank, tokens), f32),
    ]
    for _ in range(3):
        scratch.append(pltpu.VMEM((chips, per_owner, rank, wide), bf16))
        scratch.append(pltpu.VMEM((chips, per_owner, rank, narrow), bf16))
    for width in (wide, narrow):
        scratch.append(pltpu.VMEM((size_a, size_b, rank, width), bf16))
        scratch.append(pltpu.VMEM((size_b, size_a, rank, width), bf16))
    for width in (wide, narrow):
        scratch.append(pltpu.VMEM((size_b, rank, width), bf16))
        scratch.append(pltpu.VMEM((size_a, rank, width), bf16))
    scratch += [
        dma((sends,)),
        dma((2, dp_count, per_owner)),
        dma((2, tensor_count)),
        dma((2,)),
        dma((2, size_a, size_b)),
        dma((2, size_b, size_a)),
        dma((2, size_b)),
        dma((2, size_a)),
    ]
    rows = dp_count * per_owner * rank
    return pl.pallas_call(
        functools.partial(kernel, dp_count, tensor_count, sends),
        out_shape=(
            jax.ShapeDtypeStruct((tokens, wide), bf16),
            jax.ShapeDtypeStruct((per_owner, rank, wide), f32),
            jax.ShapeDtypeStruct((per_owner, rank, narrow), f32),
        ),
        in_specs=[smem] * 3 + [vmem] * 4,
        out_specs=(vmem, vmem, vmem),
        scratch_shapes=scratch,
        compiler_params=pltpu.CompilerParams(
            collective_id=0, has_side_effects=True, vmem_limit_bytes=56 * 2**20
        ),
        cost_estimate=pl.CostEstimate(
            flops=2 * rows * tokens * (3 * wide + 2 * narrow),
            bytes_accessed=2 * tokens * (2 * wide + narrow),
            transcendentals=0,
        ),
    )(counts, offsets, adapter_slot, output_gradient, hidden, adapter_down, adapter_up)


def solution(mesh):
    placed = (
        P("dp", "tensor"),
        P("dp", "tensor"),
        P("dp", None, "tensor"),
        P("dp", None, "tensor"),
        P(),
        P(),
        P(),
    )
    return jax.shard_map(
        on_device,
        mesh=mesh,
        in_specs=placed,
        out_specs=(P("dp", "tensor"), P("dp", None, "tensor"), P("dp", None, "tensor")),
        check_vma=False,
    )
```

```python
import functools
import math

import jax
import jax.numpy as jnp
from jax import lax
from jax.experimental import pallas as pl
from jax.experimental.pallas import tpu as pltpu
from jax.sharding import PartitionSpec as P

adapter_factor = 2.0
MESH = pl.DeviceIdType.MESH


def chip_grid(dp_count):
    chips = dp_count // 2
    second = max(d for d in range(1, math.isqrt(chips) + 1) if chips % d == 0)
    return chips // second, second


def kernel(
    dp_count, tensor_count, sends,
    counts, offsets, slots, og_in, hid_in, adn, aup,
    out_h, out_d, out_u,
    og, hid, gath_d, gath_u, z_up, z_dn,
    sib_d, sib_u, got_d, got_u, sum_d, sum_u,
    one_d0, one_d1, one_u0, one_u1, two_d0, two_d1, two_u0, two_u1,
    load_sem, send_sem, gath_sem, z_sem, sib_sem, one_sem0, one_sem1, two_sem0, two_sem1,
):
    size_a, size_b = chip_grid(dp_count)
    chips = size_a * size_b
    tokens = og.shape[0]
    per_owner, rank = adn.shape[0], adn.shape[1]
    me = lax.axis_index("dp")
    me_t = lax.axis_index("tensor")
    core = me % 2
    chip = me // 2
    at_a, at_b = chip // size_b, chip % size_b
    sibling = chip * 2 + (1 - core)

    def chip_of(half, first, second):
        return first * size_b + second if half == 0 else second * size_b + first

    def axes(half):
        if half == 0:
            return at_a, size_a, at_b, size_b
        return at_b, size_b, at_a, size_a

    started = []

    def push(src, dst, recv, **device):
        copy = pltpu.make_async_remote_copy(
            src_ref=src, dst_ref=dst, send_sem=send_sem.at[len(started)], recv_sem=recv,
            device_id=device, device_id_type=MESH,
        )
        copy.start()
        started.append(copy)

    def arrived(dst, recv):
        pltpu.make_async_remote_copy(
            src_ref=dst, dst_ref=dst, send_sem=send_sem.at[0], recv_sem=recv,
            device_id={"dp": sibling}, device_id_type=MESH,
        ).wait_recv()

    loads = [
        pltpu.make_async_copy(aup, gath_u.at[me], load_sem.at[0]),
        pltpu.make_async_copy(og_in, og, load_sem.at[1]),
        pltpu.make_async_copy(hid_in, hid, load_sem.at[2]),
        pltpu.make_async_copy(adn, gath_d.at[me], load_sem.at[3]),
    ]
    for load in loads:
        load.start()

    barrier = pltpu.get_barrier_semaphore()
    partners = [{"dp": sibling}]
    for off in range(1, size_a):
        partners.append({"dp": (((at_a + off) % size_a) * size_b + at_b) * 2 + core})
    for off in range(1, size_b):
        partners.append({"dp": (at_a * size_b + (at_b + off) % size_b) * 2 + core})
    for off in range(1, tensor_count):
        partners.append({"tensor": (me_t + off) % tensor_count})
    for partner in partners:
        pl.semaphore_signal(barrier, inc=1, device_id=partner, device_id_type=MESH)
    pl.semaphore_wait(barrier, len(partners))

    def gather_own(which, own, gath):
        for along_first in (True, False):
            for half in range(per_owner):
                first, n_first, second, n_second = axes(half)
                recv = gath_sem.at[which, me, half]
                for off in range(1, n_first if along_first else n_second):
                    if along_first:
                        to = chip_of(half, (first + off) % n_first, second) * 2 + core
                    else:
                        to = chip_of(half, first, (second + off) % n_second) * 2 + core
                    push(own.at[half], gath.at[me, half], recv, dp=to)
        for half in range(per_owner):
            push(own.at[half], gath.at[me, half], gath_sem.at[which, me, half], dp=sibling)

    def gather_first(which, gath):
        for half in range(per_owner):
            first, n_first, second, n_second = axes(half)
            for off in range(1, n_first):
                origin = chip_of(half, (first + off) % n_first, second) * 2 + core
                block, recv = gath.at[origin, half], gath_sem.at[which, origin, half]
                arrived(block, recv)
                for off2 in range(1, n_second):
                    to = chip_of(half, first, (second + off2) % n_second) * 2 + core
                    push(block, block, recv, dp=to)
                push(block, block, recv, dp=sibling)

    def gather_second(which, gath):
        for near in (True, False):
            for half in range(per_owner):
                first, n_first, second, n_second = axes(half)
                for off2 in range(1, n_second):
                    for off in range(0, 1) if near else range(1, n_first):
                        origin = chip_of(
                            half, (first + off) % n_first, (second + off2) % n_second
                        ) * 2 + core
                        block, recv = gath.at[origin, half], gath_sem.at[which, origin, half]
                        arrived(block, recv)
                        push(block, block, recv, dp=sibling)

    def gather_sibling(which, gath):
        for other in range(chips):
            for half in range(per_owner):
                origin = other * 2 + (1 - core)
                arrived(gath.at[origin, half], gath_sem.at[which, origin, half])

    gather_own(0, aup, gath_u)
    position = me * tokens + lax.broadcasted_iota(jnp.int32, (1, tokens), 1)
    slot_of = jnp.zeros((1, tokens), jnp.int32)
    for adapter in range(counts.shape[0]):
        low = offsets[adapter]
        inside = (position >= low) & (position < low + counts[adapter])
        slot_of = slot_of + jnp.where(inside, slots[adapter], 0)

    def tile_of(width):
        return math.gcd(width, 512)

    def partial_signal(values, gath):
        width = values.shape[1]
        tile = tile_of(width)
        rows = dp_count * per_owner * rank

        def step(at, total):
            cols = pl.ds(pl.multiple_of(at * tile, tile), tile)
            maps = gath[:, :, :, cols].reshape(rows, tile)
            return total + lax.dot_general(
                maps, values[:, cols], (((1,), (1,)), ((), ())),
                preferred_element_type=jnp.float32,
            )

        scores = lax.fori_loop(
            0, width // tile, step, jnp.zeros((rows, tokens), jnp.float32)
        ).reshape(dp_count * per_owner, rank, tokens)
        total = jnp.zeros((rank, tokens), jnp.float32)
        for slot in range(dp_count * per_owner):
            total = total + jnp.where(slot_of == slot, scores[slot], 0.0)
        return total

    def share(which, buffer, value):
        buffer[pl.ds(me_t, 1)] = value[None]
        for off in range(1, tensor_count):
            push(
                buffer.at[me_t], buffer.at[me_t], z_sem.at[which, me_t],
                tensor=(me_t + off) % tensor_count,
            )

    def shared(which, buffer):
        for off in range(1, tensor_count):
            origin = (me_t + off) % tensor_count
            arrived(buffer.at[origin], z_sem.at[which, origin])
        total = buffer[0]
        for origin in range(1, tensor_count):
            total = total + buffer[origin]
        return total.astype(jnp.bfloat16).astype(jnp.float32)

    def spread(signal, numbers):
        return jnp.concatenate(
            [jnp.where(slot_of == number, signal, 0.0) for number in numbers], axis=0
        )

    def numbers_of(which_core):
        return [
            (other * 2 + which_core) * per_owner + half
            for other in range(chips)
            for half in range(per_owner)
        ]

    def sums_sibling(which, signal, values, sib, got):
        rows = spread(signal, numbers_of(1 - core)).astype(jnp.bfloat16)
        width = values.shape[1]
        tile = tile_of(width)

        def step(at, _):
            cols = pl.ds(pl.multiple_of(at * tile, tile), tile)
            term = jnp.dot(rows, values[:, cols], preferred_element_type=jnp.float32)
            sib[:, :, :, cols] = term.astype(jnp.bfloat16).reshape(chips, per_owner, rank, tile)
            return 0

        lax.fori_loop(0, width // tile, step, 0)
        push(sib, got, sib_sem.at[which], dp=sibling)

    def sums_first(which, signal, values, got, total, one):
        rows = spread(signal, numbers_of(core)).astype(jnp.bfloat16)
        width = values.shape[1]
        tile = tile_of(width)
        arrived(got, sib_sem.at[which])

        def step(at, _):
            cols = pl.ds(pl.multiple_of(at * tile, tile), tile)
            term = jnp.dot(rows, values[:, cols], preferred_element_type=jnp.float32)
            term = term.reshape(chips, per_owner, rank, tile)
            term = term + got[:, :, :, cols].astype(jnp.float32)
            total[:, :, :, cols] = term.astype(jnp.bfloat16)
            return 0

        lax.fori_loop(0, width // tile, step, 0)
        sems = (one_sem0, one_sem1)
        for far in (True, False):
            for half in range(per_owner):
                first, n_first, second, n_second = axes(half)
                for off in range(1, n_first):
                    peer = (first + off) % n_first
                    to = chip_of(half, peer, second) * 2 + core
                    for off2 in range(1, n_second) if far else range(0, 1):
                        owner_second = (second + off2) % n_second
                        push(
                            total.at[chip_of(half, peer, owner_second), half],
                            one[half].at[first, owner_second],
                            sems[half].at[which, first, owner_second],
                            dp=to,
                        )

    def sums_second(which, total, one, two):
        sems, sems2 = (one_sem0, one_sem1), (two_sem0, two_sem1)
        for half in range(per_owner):
            first, n_first, second, n_second = axes(half)
            for off2 in range(1, n_second):
                owner_second = (second + off2) % n_second
                owner = chip_of(half, first, owner_second)
                value = total[owner, half].astype(jnp.float32)
                for off in range(1, n_first):
                    peer = (first + off) % n_first
                    arrived(
                        one[half].at[peer, owner_second],
                        sems[half].at[which, peer, owner_second],
                    )
                    value = value + one[half][peer, owner_second].astype(jnp.float32)
                total[pl.ds(owner, 1), half] = value.astype(jnp.bfloat16)[None]
                push(
                    total.at[owner, half], two[half].at[second],
                    sems2[half].at[which, second], dp=owner * 2 + core,
                )

    def sums_last(which, total, one, two, out):
        sems, sems2 = (one_sem0, one_sem1), (two_sem0, two_sem1)
        for half in range(per_owner):
            first, n_first, second, n_second = axes(half)
            value = total[chip, half].astype(jnp.float32)
            for off in range(1, n_first):
                peer = (first + off) % n_first
                arrived(one[half].at[peer, second], sems[half].at[which, peer, second])
                value = value + one[half][peer, second].astype(jnp.float32)
            for off2 in range(1, n_second):
                peer = (second + off2) % n_second
                arrived(two[half].at[peer], sems2[half].at[which, peer])
                value = value + two[half][peer].astype(jnp.float32)
            number = me * per_owner + half
            held = jnp.zeros((1, 1), jnp.int32)
            for adapter in range(counts.shape[0]):
                mine = jnp.full((1, 1), slots[adapter], jnp.int32) == number
                held = held + jnp.where(mine, counts[adapter], 0)
            out[half] = value * (adapter_factor / held.astype(jnp.float32))

    one_d, one_u = (one_d0, one_d1), (one_u0, one_u1)
    two_d, two_u = (two_d0, two_d1), (two_u0, two_u1)

    gather_first(0, gath_u)
    gather_own(1, adn, gath_d)
    gather_second(0, gath_u)
    gather_sibling(0, gath_u)
    loads[0].wait()
    loads[1].wait()
    share(0, z_up, partial_signal(og, gath_u))
    loads[2].wait()
    up_signal = shared(0, z_up)
    sums_sibling(0, up_signal, hid, sib_d, got_d)
    gather_first(1, gath_d)
    sums_first(0, up_signal, hid, got_d, sum_d, one_d)
    gather_second(1, gath_d)
    gather_sibling(1, gath_d)
    loads[3].wait()
    share(1, z_dn, partial_signal(hid, gath_d))

    all_rows = dp_count * per_owner * rank
    tokens_by_row = spread(up_signal, range(dp_count * per_owner)).T.astype(jnp.bfloat16)
    tile = tile_of(hid.shape[1])

    def hidden_step(at, _):
        cols = pl.ds(pl.multiple_of(at * tile, tile), tile)
        maps = gath_d[:, :, :, cols].reshape(all_rows, tile)
        term = jnp.dot(tokens_by_row, maps, preferred_element_type=jnp.float32)
        out_h[:, cols] = (adapter_factor * term).astype(out_h.dtype)
        return 0

    lax.fori_loop(0, hid.shape[1] // tile, hidden_step, 0)

    down_signal = shared(1, z_dn)
    sums_sibling(1, down_signal, og, sib_u, got_u)
    sums_first(1, down_signal, og, got_u, sum_u, one_u)
    sums_second(0, sum_d, one_d, two_d)
    sums_second(1, sum_u, one_u, two_u)
    sums_last(0, sum_d, one_d, two_d, out_d)
    sums_last(1, sum_u, one_u, two_u, out_u)
    for copy in started:
        copy.wait_send()
    assert len(started) == sends, (len(started), sends)


def send_count(dp_count, tensor_count, per_owner):
    size_a, size_b = chip_grid(dp_count)
    total = 2 * (tensor_count - 1) + 2
    for half in range(per_owner):
        n_first, n_second = (size_a, size_b) if half == 0 else (size_b, size_a)
        own = n_first + n_second - 1
        relayed = (n_first - 1) * n_second + (n_second - 1) * n_first
        back = (n_first - 1) * n_second + (n_second - 1)
        total += 2 * (own + relayed + back)
    return total


def on_device(output_gradient, hidden, adapter_down, adapter_up, counts, offsets, adapter_slot):
    dp_count, tensor_count = lax.axis_size("dp"), lax.axis_size("tensor")
    size_a, size_b = chip_grid(dp_count)
    chips = size_a * size_b
    per_owner, rank, wide = adapter_down.shape
    narrow = adapter_up.shape[2]
    tokens = hidden.shape[0]
    sends = send_count(dp_count, tensor_count, per_owner)
    bf16, f32 = jnp.bfloat16, jnp.float32
    dma = pltpu.SemaphoreType.DMA
    vmem = pl.BlockSpec(memory_space=pltpu.VMEM)
    smem = pl.BlockSpec(memory_space=pltpu.SMEM)
    scratch = [
        pltpu.VMEM((tokens, narrow), bf16),
        pltpu.VMEM((tokens, wide), bf16),
        pltpu.VMEM((dp_count, per_owner, rank, wide), bf16),
        pltpu.VMEM((dp_count, per_owner, rank, narrow), bf16),
        pltpu.VMEM((tensor_count, rank, tokens), f32),
        pltpu.VMEM((tensor_count, rank, tokens), f32),
    ]
    for _ in range(3):
        scratch.append(pltpu.VMEM((chips, per_owner, rank, wide), bf16))
        scratch.append(pltpu.VMEM((chips, per_owner, rank, narrow), bf16))
    for width in (wide, narrow):
        scratch.append(pltpu.VMEM((size_a, size_b, rank, width), bf16))
        scratch.append(pltpu.VMEM((size_b, size_a, rank, width), bf16))
    for width in (wide, narrow):
        scratch.append(pltpu.VMEM((size_b, rank, width), bf16))
        scratch.append(pltpu.VMEM((size_a, rank, width), bf16))
    scratch += [
        dma((4,)),
        dma((sends,)),
        dma((2, dp_count, per_owner)),
        dma((2, tensor_count)),
        dma((2,)),
        dma((2, size_a, size_b)),
        dma((2, size_b, size_a)),
        dma((2, size_b)),
        dma((2, size_a)),
    ]
    rows = dp_count * per_owner * rank
    return pl.pallas_call(
        functools.partial(kernel, dp_count, tensor_count, sends),
        out_shape=(
            pltpu.VMEM((tokens, wide), bf16),
            pltpu.VMEM((per_owner, rank, wide), f32),
            pltpu.VMEM((per_owner, rank, narrow), f32),
        ),
        in_specs=[smem] * 3 + [pl.BlockSpec(memory_space=pl.ANY)] * 4,
        out_specs=(vmem, vmem, vmem),
        scratch_shapes=scratch,
        compiler_params=pltpu.CompilerParams(
            collective_id=0, has_side_effects=True, vmem_limit_bytes=48 * 2**20
        ),
        cost_estimate=pl.CostEstimate(
            flops=2 * rows * tokens * (3 * wide + 2 * narrow),
            bytes_accessed=2 * tokens * (2 * wide + narrow),
            transcendentals=0,
        ),
    )(counts, offsets, adapter_slot, output_gradient, hidden, adapter_down, adapter_up)


def solution(mesh):
    placed = (
        P("dp", "tensor"),
        P("dp", "tensor"),
        P("dp", None, "tensor"),
        P("dp", None, "tensor"),
        P(),
        P(),
        P(),
    )
    return jax.shard_map(
        on_device,
        mesh=mesh,
        in_specs=placed,
        out_specs=(P("dp", "tensor"), P("dp", None, "tensor"), P("dp", None, "tensor")),
        check_vma=False,
    )
```

```python
import functools
import math

import jax
import jax.numpy as jnp
from jax import lax
from jax.experimental import pallas as pl
from jax.experimental.pallas import tpu as pltpu
from jax.sharding import PartitionSpec as P

adapter_factor = 2.0
MESH = pl.DeviceIdType.MESH


def chip_grid(dp_count):
    chips = dp_count // 2
    second = max(d for d in range(1, math.isqrt(chips) + 1) if chips % d == 0)
    return chips // second, second


def kernel(
    dp_count, tensor_count, sends,
    counts_in, offsets_in, slots_in, og_in, hid_in, adn, aup,
    out_h, out_d, out_u,
    counts, offsets, slots, og, hid, gath_d, gath_u, z_up, z_dn,
    sib_d, sib_u, got_d, got_u, sum_d, sum_u,
    one_d0, one_d1, one_u0, one_u1, two_d0, two_d1, two_u0, two_u1,
    load_sem, send_sem, gath_sem, z_sem, sib_sem, one_sem0, one_sem1, two_sem0, two_sem1,
):
    size_a, size_b = chip_grid(dp_count)
    chips = size_a * size_b
    tokens = og.shape[0]
    per_owner, rank = adn.shape[0], adn.shape[1]
    me = lax.axis_index("dp")
    me_t = lax.axis_index("tensor")
    core = me % 2
    chip = me // 2
    at_a, at_b = chip // size_b, chip % size_b
    sibling = chip * 2 + (1 - core)

    def chip_of(half, first, second):
        return first * size_b + second if half == 0 else second * size_b + first

    def axes(half):
        if half == 0:
            return at_a, size_a, at_b, size_b
        return at_b, size_b, at_a, size_a

    started = []

    def push(src, dst, recv, **device):
        copy = pltpu.make_async_remote_copy(
            src_ref=src, dst_ref=dst, send_sem=send_sem.at[len(started)], recv_sem=recv,
            device_id=device, device_id_type=MESH,
        )
        copy.start()
        started.append(copy)

    def arrived(dst, recv):
        pltpu.make_async_remote_copy(
            src_ref=dst, dst_ref=dst, send_sem=send_sem.at[0], recv_sem=recv,
            device_id={"dp": sibling}, device_id_type=MESH,
        ).wait_recv()

    loads = [
        pltpu.make_async_copy(aup, gath_u.at[me], load_sem.at[0]),
        pltpu.make_async_copy(og_in, og, load_sem.at[1]),
        pltpu.make_async_copy(hid_in, hid, load_sem.at[2]),
        pltpu.make_async_copy(adn, gath_d.at[me], load_sem.at[3]),
        pltpu.make_async_copy(counts_in, counts, load_sem.at[4]),
        pltpu.make_async_copy(offsets_in, offsets, load_sem.at[5]),
        pltpu.make_async_copy(slots_in, slots, load_sem.at[6]),
    ]
    for load in loads:
        load.start()

    barrier = pltpu.get_barrier_semaphore()
    partners = [{"dp": sibling}]
    for off in range(1, size_a):
        partners.append({"dp": (((at_a + off) % size_a) * size_b + at_b) * 2 + core})
    for off in range(1, size_b):
        partners.append({"dp": (at_a * size_b + (at_b + off) % size_b) * 2 + core})
    for off in range(1, tensor_count):
        partners.append({"tensor": (me_t + off) % tensor_count})
    for partner in partners:
        pl.semaphore_signal(barrier, inc=1, device_id=partner, device_id_type=MESH)
    pl.semaphore_wait(barrier, len(partners))

    def gather_own(which, own, gath):
        for along_first in (True, False):
            for half in range(per_owner):
                first, n_first, second, n_second = axes(half)
                recv = gath_sem.at[which, me, half]
                for off in range(1, n_first if along_first else n_second):
                    if along_first:
                        to = chip_of(half, (first + off) % n_first, second) * 2 + core
                    else:
                        to = chip_of(half, first, (second + off) % n_second) * 2 + core
                    push(own.at[half], gath.at[me, half], recv, dp=to)
        for half in range(per_owner):
            push(own.at[half], gath.at[me, half], gath_sem.at[which, me, half], dp=sibling)

    def gather_first(which, gath):
        for half in range(per_owner):
            first, n_first, second, n_second = axes(half)
            for off in range(1, n_first):
                origin = chip_of(half, (first + off) % n_first, second) * 2 + core
                block, recv = gath.at[origin, half], gath_sem.at[which, origin, half]
                arrived(block, recv)
                for off2 in range(1, n_second):
                    to = chip_of(half, first, (second + off2) % n_second) * 2 + core
                    push(block, block, recv, dp=to)
                push(block, block, recv, dp=sibling)

    def gather_second(which, gath):
        for near in (True, False):
            for half in range(per_owner):
                first, n_first, second, n_second = axes(half)
                for off2 in range(1, n_second):
                    for off in range(0, 1) if near else range(1, n_first):
                        origin = chip_of(
                            half, (first + off) % n_first, (second + off2) % n_second
                        ) * 2 + core
                        block, recv = gath.at[origin, half], gath_sem.at[which, origin, half]
                        arrived(block, recv)
                        push(block, block, recv, dp=sibling)

    def gather_sibling(which, gath):
        for other in range(chips):
            for half in range(per_owner):
                origin = other * 2 + (1 - core)
                arrived(gath.at[origin, half], gath_sem.at[which, origin, half])

    gather_own(0, aup, gath_u)
    for load in loads[4:]:
        load.wait()
    position = me * tokens + lax.broadcasted_iota(jnp.int32, (1, tokens), 1)
    slot_of = jnp.zeros((1, tokens), jnp.int32)
    for adapter in range(counts.shape[0]):
        low = offsets[adapter]
        inside = (position >= low) & (position < low + counts[adapter])
        slot_of = slot_of + jnp.where(inside, slots[adapter], 0)

    def tile_of(width):
        return math.gcd(width, 1024)

    def partial_signal(values, gath):
        rows = dp_count * per_owner * rank
        scores = lax.dot_general(
            gath[...].reshape(rows, values.shape[1]), values[...], (((1,), (1,)), ((), ())),
            preferred_element_type=jnp.float32,
        ).reshape(dp_count * per_owner, rank, tokens)
        total = jnp.zeros((rank, tokens), jnp.float32)
        for slot in range(dp_count * per_owner):
            total = total + jnp.where(slot_of == slot, scores[slot], 0.0)
        return total

    def share(which, buffer, value):
        buffer[pl.ds(me_t, 1)] = value[None]
        for off in range(1, tensor_count):
            push(
                buffer.at[me_t], buffer.at[me_t], z_sem.at[which, me_t],
                tensor=(me_t + off) % tensor_count,
            )

    def shared(which, buffer):
        for off in range(1, tensor_count):
            origin = (me_t + off) % tensor_count
            arrived(buffer.at[origin], z_sem.at[which, origin])
        total = buffer[0]
        for origin in range(1, tensor_count):
            total = total + buffer[origin]
        return total.astype(jnp.bfloat16).astype(jnp.float32)

    def spread(signal, numbers):
        return jnp.concatenate(
            [jnp.where(slot_of == number, signal, 0.0) for number in numbers], axis=0
        )

    def numbers_of(which_core):
        return [
            (other * 2 + which_core) * per_owner + half
            for other in range(chips)
            for half in range(per_owner)
        ]

    def sums_sibling(which, signal, values, sib, got):
        rows = spread(signal, numbers_of(1 - core)).astype(jnp.bfloat16)
        width = values.shape[1]
        tile = tile_of(width)

        for at in range(width // tile):
            cols = slice(at * tile, (at + 1) * tile)
            term = jnp.dot(rows, values[:, cols], preferred_element_type=jnp.float32)
            sib[:, :, :, cols] = term.astype(jnp.bfloat16).reshape(chips, per_owner, rank, tile)

        push(sib, got, sib_sem.at[which], dp=sibling)

    def sums_first(which, signal, values, got, total, one):
        rows = spread(signal, numbers_of(core)).astype(jnp.bfloat16)
        width = values.shape[1]
        tile = tile_of(width)
        arrived(got, sib_sem.at[which])

        for at in range(width // tile):
            cols = slice(at * tile, (at + 1) * tile)
            term = jnp.dot(rows, values[:, cols], preferred_element_type=jnp.float32)
            term = term.reshape(chips, per_owner, rank, tile)
            term = term + got[:, :, :, cols].astype(jnp.float32)
            total[:, :, :, cols] = term.astype(jnp.bfloat16)

        sems = (one_sem0, one_sem1)
        for far in (True, False):
            for half in range(per_owner):
                first, n_first, second, n_second = axes(half)
                for off in range(1, n_first):
                    peer = (first + off) % n_first
                    to = chip_of(half, peer, second) * 2 + core
                    for off2 in range(1, n_second) if far else range(0, 1):
                        owner_second = (second + off2) % n_second
                        push(
                            total.at[chip_of(half, peer, owner_second), half],
                            one[half].at[first, owner_second],
                            sems[half].at[which, first, owner_second],
                            dp=to,
                        )

    def sums_second(which, total, one, two):
        sems, sems2 = (one_sem0, one_sem1), (two_sem0, two_sem1)
        for half in range(per_owner):
            first, n_first, second, n_second = axes(half)
            for off2 in range(1, n_second):
                owner_second = (second + off2) % n_second
                owner = chip_of(half, first, owner_second)
                value = total[owner, half].astype(jnp.float32)
                for off in range(1, n_first):
                    peer = (first + off) % n_first
                    arrived(
                        one[half].at[peer, owner_second],
                        sems[half].at[which, peer, owner_second],
                    )
                    value = value + one[half][peer, owner_second].astype(jnp.float32)
                total[pl.ds(owner, 1), half] = value.astype(jnp.bfloat16)[None]
                push(
                    total.at[owner, half], two[half].at[second],
                    sems2[half].at[which, second], dp=owner * 2 + core,
                )

    def sums_last(which, total, one, two, out):
        sems, sems2 = (one_sem0, one_sem1), (two_sem0, two_sem1)
        for half in range(per_owner):
            first, n_first, second, n_second = axes(half)
            value = total[chip, half].astype(jnp.float32)
            for off in range(1, n_first):
                peer = (first + off) % n_first
                arrived(one[half].at[peer, second], sems[half].at[which, peer, second])
                value = value + one[half][peer, second].astype(jnp.float32)
            for off2 in range(1, n_second):
                peer = (second + off2) % n_second
                arrived(two[half].at[peer], sems2[half].at[which, peer])
                value = value + two[half][peer].astype(jnp.float32)
            number = me * per_owner + half
            held = jnp.zeros((1, 1), jnp.int32)
            for adapter in range(counts.shape[0]):
                mine = jnp.full((1, 1), slots[adapter], jnp.int32) == number
                held = held + jnp.where(mine, counts[adapter], 0)
            out[half] = value * (adapter_factor / held.astype(jnp.float32))

    one_d, one_u = (one_d0, one_d1), (one_u0, one_u1)
    two_d, two_u = (two_d0, two_d1), (two_u0, two_u1)

    gather_first(0, gath_u)
    gather_own(1, adn, gath_d)
    gather_second(0, gath_u)
    gather_sibling(0, gath_u)
    loads[0].wait()
    loads[1].wait()
    share(0, z_up, partial_signal(og, gath_u))
    gather_first(1, gath_d)
    loads[2].wait()
    up_signal = shared(0, z_up)
    sums_sibling(0, up_signal, hid, sib_d, got_d)
    sums_first(0, up_signal, hid, got_d, sum_d, one_d)
    gather_second(1, gath_d)
    gather_sibling(1, gath_d)
    loads[3].wait()
    share(1, z_dn, partial_signal(hid, gath_d))

    all_rows = dp_count * per_owner * rank
    tokens_by_row = spread(up_signal, range(dp_count * per_owner)).T.astype(jnp.bfloat16)
    tile = tile_of(hid.shape[1])

    for at in range(hid.shape[1] // tile):
        cols = slice(at * tile, (at + 1) * tile)
        maps = gath_d[:, :, :, cols].reshape(all_rows, tile)
        term = jnp.dot(tokens_by_row, maps, preferred_element_type=jnp.float32)
        out_h[:, cols] = (adapter_factor * term).astype(out_h.dtype)

    down_signal = shared(1, z_dn)
    sums_sibling(1, down_signal, og, sib_u, got_u)
    sums_first(1, down_signal, og, got_u, sum_u, one_u)
    sums_second(0, sum_d, one_d, two_d)
    sums_second(1, sum_u, one_u, two_u)
    sums_last(0, sum_d, one_d, two_d, out_d)
    sums_last(1, sum_u, one_u, two_u, out_u)
    for copy in started:
        copy.wait_send()
    assert len(started) == sends, (len(started), sends)


def write_out(h, d, u, out_h, out_d, out_u, sem):
    copies = [
        pltpu.make_async_copy(src, dst, sem.at[at])
        for at, (src, dst) in enumerate(((h, out_h), (d, out_d), (u, out_u)))
    ]
    for copy in copies:
        copy.start()
    for copy in copies:
        copy.wait()


def send_count(dp_count, tensor_count, per_owner):
    size_a, size_b = chip_grid(dp_count)
    total = 2 * (tensor_count - 1) + 2
    for half in range(per_owner):
        n_first, n_second = (size_a, size_b) if half == 0 else (size_b, size_a)
        own = n_first + n_second - 1
        relayed = (n_first - 1) * n_second + (n_second - 1) * n_first
        back = (n_first - 1) * n_second + (n_second - 1)
        total += 2 * (own + relayed + back)
    return total


def on_device(output_gradient, hidden, adapter_down, adapter_up, counts, offsets, adapter_slot):
    dp_count, tensor_count = lax.axis_size("dp"), lax.axis_size("tensor")
    size_a, size_b = chip_grid(dp_count)
    chips = size_a * size_b
    per_owner, rank, wide = adapter_down.shape
    narrow = adapter_up.shape[2]
    tokens = hidden.shape[0]
    sends = send_count(dp_count, tensor_count, per_owner)
    bf16, f32 = jnp.bfloat16, jnp.float32
    dma = pltpu.SemaphoreType.DMA
    vmem = pl.BlockSpec(memory_space=pltpu.VMEM)
    any_space = pl.BlockSpec(memory_space=pl.ANY)
    scratch = [
        pltpu.SMEM(counts.shape, jnp.int32),
        pltpu.SMEM(offsets.shape, jnp.int32),
        pltpu.SMEM(adapter_slot.shape, jnp.int32),
        pltpu.VMEM((tokens, narrow), bf16),
        pltpu.VMEM((tokens, wide), bf16),
        pltpu.VMEM((dp_count, per_owner, rank, wide), bf16),
        pltpu.VMEM((dp_count, per_owner, rank, narrow), bf16),
        pltpu.VMEM((tensor_count, rank, tokens), f32),
        pltpu.VMEM((tensor_count, rank, tokens), f32),
    ]
    for _ in range(3):
        scratch.append(pltpu.VMEM((chips, per_owner, rank, wide), bf16))
        scratch.append(pltpu.VMEM((chips, per_owner, rank, narrow), bf16))
    for width in (wide, narrow):
        scratch.append(pltpu.VMEM((size_a, size_b, rank, width), bf16))
        scratch.append(pltpu.VMEM((size_b, size_a, rank, width), bf16))
    for width in (wide, narrow):
        scratch.append(pltpu.VMEM((size_b, rank, width), bf16))
        scratch.append(pltpu.VMEM((size_a, rank, width), bf16))
    scratch += [
        dma((7,)),
        dma((sends,)),
        dma((2, dp_count, per_owner)),
        dma((2, tensor_count)),
        dma((2,)),
        dma((2, size_a, size_b)),
        dma((2, size_b, size_a)),
        dma((2, size_b)),
        dma((2, size_a)),
    ]
    rows = dp_count * per_owner * rank
    results = pl.pallas_call(
        functools.partial(kernel, dp_count, tensor_count, sends),
        out_shape=(
            pltpu.VMEM((tokens, wide), bf16),
            pltpu.VMEM((per_owner, rank, wide), f32),
            pltpu.VMEM((per_owner, rank, narrow), f32),
        ),
        in_specs=[any_space] * 7,
        out_specs=(vmem, vmem, vmem),
        scratch_shapes=scratch,
        compiler_params=pltpu.CompilerParams(
            collective_id=0, has_side_effects=True, vmem_limit_bytes=48 * 2**20
        ),
        cost_estimate=pl.CostEstimate(
            flops=2 * rows * tokens * (3 * wide + 2 * narrow),
            bytes_accessed=2 * tokens * (2 * wide + narrow),
            transcendentals=0,
        ),
    )(*(
        pltpu.with_memory_space_constraint(array, pltpu.HBM)
        for array in (
            counts, offsets, adapter_slot, output_gradient, hidden, adapter_down, adapter_up
        )
    ))
    return pl.pallas_call(
        write_out,
        out_shape=tuple(jax.ShapeDtypeStruct(r.shape, r.dtype) for r in results),
        in_specs=[any_space] * 3,
        out_specs=(any_space,) * 3,
        scratch_shapes=[dma((3,))],
        cost_estimate=pl.CostEstimate(
            flops=0, bytes_accessed=2 * tokens * wide, transcendentals=0
        ),
    )(*results)


def solution(mesh):
    placed = (
        P("dp", "tensor"),
        P("dp", "tensor"),
        P("dp", None, "tensor"),
        P("dp", None, "tensor"),
        P(),
        P(),
        P(),
    )
    return jax.shard_map(
        on_device,
        mesh=mesh,
        in_specs=placed,
        out_specs=(P("dp", "tensor"), P("dp", None, "tensor"), P("dp", None, "tensor")),
        check_vma=False,
    )
```

```python
import functools
import math

import jax
import jax.numpy as jnp
from jax import lax
from jax.experimental import pallas as pl
from jax.experimental.pallas import tpu as pltpu
from jax.sharding import PartitionSpec as P

adapter_factor = 2.0
MESH = pl.DeviceIdType.MESH


def chip_grid(dp_count):
    chips = dp_count // 2
    second = max(d for d in range(1, math.isqrt(chips) + 1) if chips % d == 0)
    return chips // second, second


def kernel(
    dp_count, tensor_count, sends, pieces,
    counts_in, offsets_in, slots_in, og_in, hid_in, adn, aup,
    out_h, out_d, out_u,
    counts, offsets, slots, og, hid, gath_d, gath_u, z_up, z_dn,
    sib_d, sib_u, got_d, got_u, sum_d, sum_u,
    one_d0, one_d1, one_u0, one_u1, two_d0, two_d1, two_u0, two_u1,
    load_sem, send_sem, gath_sem, z_sem, sib_sem, one_sem0, one_sem1, two_sem0, two_sem1,
):
    size_a, size_b = chip_grid(dp_count)
    chips = size_a * size_b
    tokens = og.shape[0]
    per_owner, rank = adn.shape[0], adn.shape[1]
    me = lax.axis_index("dp")
    me_t = lax.axis_index("tensor")
    core = me % 2
    chip = me // 2
    at_a, at_b = chip // size_b, chip % size_b
    sibling = chip * 2 + (1 - core)

    def chip_of(half, first, second):
        return first * size_b + second if half == 0 else second * size_b + first

    def axes(half):
        if half == 0:
            return at_a, size_a, at_b, size_b
        return at_b, size_b, at_a, size_a

    started = []

    def push(src, dst, recv, **device):
        copy = pltpu.make_async_remote_copy(
            src_ref=src, dst_ref=dst, send_sem=send_sem.at[len(started)], recv_sem=recv,
            device_id=device, device_id_type=MESH,
        )
        copy.start()
        started.append(copy)

    def arrived(dst, recv):
        pltpu.make_async_remote_copy(
            src_ref=dst, dst_ref=dst, send_sem=send_sem.at[0], recv_sem=recv,
            device_id={"dp": sibling}, device_id_type=MESH,
        ).wait_recv()

    loads = [
        pltpu.make_async_copy(aup, gath_u.at[me], load_sem.at[0]),
        pltpu.make_async_copy(og_in, og, load_sem.at[1]),
        pltpu.make_async_copy(hid_in, hid, load_sem.at[2]),
        pltpu.make_async_copy(adn, gath_d.at[me], load_sem.at[3]),
        pltpu.make_async_copy(counts_in, counts, load_sem.at[4]),
        pltpu.make_async_copy(offsets_in, offsets, load_sem.at[5]),
        pltpu.make_async_copy(slots_in, slots, load_sem.at[6]),
    ]
    for load in loads:
        load.start()

    barrier = pltpu.get_barrier_semaphore()
    partners = [{"dp": sibling}]
    for off in range(1, size_a):
        partners.append({"dp": (((at_a + off) % size_a) * size_b + at_b) * 2 + core})
    for off in range(1, size_b):
        partners.append({"dp": (at_a * size_b + (at_b + off) % size_b) * 2 + core})
    for off in range(1, tensor_count):
        partners.append({"tensor": (me_t + off) % tensor_count})
    for partner in partners:
        pl.semaphore_signal(barrier, inc=1, device_id=partner, device_id_type=MESH)
    pl.semaphore_wait(barrier, len(partners))

    def gather_own(which, own, gath):
        for along_first in (True, False):
            for half in range(per_owner):
                first, n_first, second, n_second = axes(half)
                recv = gath_sem.at[which, me, half]
                for off in range(1, n_first if along_first else n_second):
                    if along_first:
                        to = chip_of(half, (first + off) % n_first, second) * 2 + core
                    else:
                        to = chip_of(half, first, (second + off) % n_second) * 2 + core
                    push(own.at[half], gath.at[me, half], recv, dp=to)
        for half in range(per_owner):
            push(own.at[half], gath.at[me, half], gath_sem.at[which, me, half], dp=sibling)

    def gather_first(which, gath):
        for half in range(per_owner):
            first, n_first, second, n_second = axes(half)
            for off in range(1, n_first):
                origin = chip_of(half, (first + off) % n_first, second) * 2 + core
                block, recv = gath.at[origin, half], gath_sem.at[which, origin, half]
                arrived(block, recv)
                for off2 in range(1, n_second):
                    to = chip_of(half, first, (second + off2) % n_second) * 2 + core
                    push(block, block, recv, dp=to)
                push(block, block, recv, dp=sibling)

    def gather_second(which, gath, near):
        for half in range(per_owner):
            first, n_first, second, n_second = axes(half)
            for off2 in range(1, n_second):
                for off in range(0, 1) if near else range(1, n_first):
                    origin = chip_of(
                        half, (first + off) % n_first, (second + off2) % n_second
                    ) * 2 + core
                    block, recv = gath.at[origin, half], gath_sem.at[which, origin, half]
                    arrived(block, recv)
                    push(block, block, recv, dp=sibling)

    def gather_sibling(which, gath):
        for other in range(chips):
            for half in range(per_owner):
                origin = other * 2 + (1 - core)
                arrived(gath.at[origin, half], gath_sem.at[which, origin, half])

    gather_own(0, aup, gath_u)
    for load in loads[4:]:
        load.wait()
    position = me * tokens + lax.broadcasted_iota(jnp.int32, (1, tokens), 1)
    slot_of = jnp.zeros((1, tokens), jnp.int32)
    for adapter in range(counts.shape[0]):
        low = offsets[adapter]
        inside = (position >= low) & (position < low + counts[adapter])
        slot_of = slot_of + jnp.where(inside, slots[adapter], 0)

    def tile_of(width):
        return math.gcd(width, 1024)

    def partial_signal(values, gath):
        rows = dp_count * per_owner * rank
        scores = lax.dot_general(
            gath[...].reshape(rows, values.shape[1]), values[...], (((1,), (1,)), ((), ())),
            preferred_element_type=jnp.float32,
        ).reshape(dp_count * per_owner, rank, tokens)
        total = jnp.zeros((rank, tokens), jnp.float32)
        for slot in range(dp_count * per_owner):
            total = total + jnp.where(slot_of == slot, scores[slot], 0.0)
        return total

    def share(which, buffer, value):
        buffer[pl.ds(me_t, 1)] = value[None]
        for off in range(1, tensor_count):
            push(
                buffer.at[me_t], buffer.at[me_t], z_sem.at[which, me_t],
                tensor=(me_t + off) % tensor_count,
            )

    def shared(which, buffer):
        for off in range(1, tensor_count):
            origin = (me_t + off) % tensor_count
            arrived(buffer.at[origin], z_sem.at[which, origin])
        total = buffer[0]
        for origin in range(1, tensor_count):
            total = total + buffer[origin]
        return total.astype(jnp.bfloat16).astype(jnp.float32)

    def spread(signal, numbers):
        return jnp.concatenate(
            [jnp.where(slot_of == number, signal, 0.0) for number in numbers], axis=0
        )

    def numbers_of(which_core):
        return [
            (other * 2 + which_core) * per_owner + half
            for other in range(chips)
            for half in range(per_owner)
        ]

    def piece_of(which, piece, width):
        return pl.ds(piece * (width // pieces[which]), width // pieces[which])

    def gradient_rows(which_core, signal):
        return spread(signal, numbers_of(which_core)).astype(jnp.bfloat16)

    def tiles(which, piece, width):
        size = width // pieces[which]
        tile = math.gcd(size, 1024)
        return [pl.ds(piece * size + at, tile) for at in range(0, size, tile)]

    def sums_sibling(which, piece, rows, values, sib, got):
        for cols in tiles(which, piece, values.shape[1]):
            term = jnp.dot(rows, values[:, cols], preferred_element_type=jnp.float32)
            sib[:, :, :, cols] = term.astype(jnp.bfloat16).reshape(
                chips, per_owner, rank, cols.size
            )
        part = piece_of(which, piece, values.shape[1])
        push(
            sib.at[:, :, :, part], got.at[:, :, :, part], sib_sem.at[which, piece], dp=sibling
        )

    def sums_first(which, piece, rows, values, got, total, one):
        part = piece_of(which, piece, values.shape[1])
        arrived(got.at[:, :, :, part], sib_sem.at[which, piece])
        for cols in tiles(which, piece, values.shape[1]):
            term = jnp.dot(rows, values[:, cols], preferred_element_type=jnp.float32)
            term = term.reshape(chips, per_owner, rank, cols.size)
            term = term + got[:, :, :, cols].astype(jnp.float32)
            total[:, :, :, cols] = term.astype(jnp.bfloat16)
        sems = (one_sem0, one_sem1)
        for far in (True, False):
            for half in range(per_owner):
                first, n_first, second, n_second = axes(half)
                for off in range(1, n_first):
                    peer = (first + off) % n_first
                    to = chip_of(half, peer, second) * 2 + core
                    for off2 in range(1, n_second) if far else range(0, 1):
                        owner_second = (second + off2) % n_second
                        push(
                            total.at[chip_of(half, peer, owner_second), half, :, part],
                            one[half].at[first, owner_second, :, part],
                            sems[half].at[which, piece, first, owner_second],
                            dp=to,
                        )

    def sums_second(which, piece, total, one, two):
        part = piece_of(which, piece, total.shape[3])
        sems, sems2 = (one_sem0, one_sem1), (two_sem0, two_sem1)
        for half in range(per_owner):
            first, n_first, second, n_second = axes(half)
            for off2 in range(1, n_second):
                owner_second = (second + off2) % n_second
                owner = chip_of(half, first, owner_second)
                value = total[owner, half, :, part].astype(jnp.float32)
                for off in range(1, n_first):
                    peer = (first + off) % n_first
                    arrived(
                        one[half].at[peer, owner_second, :, part],
                        sems[half].at[which, piece, peer, owner_second],
                    )
                    value = value + one[half][peer, owner_second, :, part].astype(jnp.float32)
                total[pl.ds(owner, 1), half, :, part] = value.astype(jnp.bfloat16)[None]
                push(
                    total.at[owner, half, :, part], two[half].at[second, :, part],
                    sems2[half].at[which, piece, second], dp=owner * 2 + core,
                )

    def sums_last(which, piece, total, one, two, out):
        part = piece_of(which, piece, total.shape[3])
        sems, sems2 = (one_sem0, one_sem1), (two_sem0, two_sem1)
        for half in range(per_owner):
            first, n_first, second, n_second = axes(half)
            value = total[chip, half, :, part].astype(jnp.float32)
            for off in range(1, n_first):
                peer = (first + off) % n_first
                arrived(
                    one[half].at[peer, second, :, part],
                    sems[half].at[which, piece, peer, second],
                )
                value = value + one[half][peer, second, :, part].astype(jnp.float32)
            for off2 in range(1, n_second):
                peer = (second + off2) % n_second
                arrived(two[half].at[peer, :, part], sems2[half].at[which, piece, peer])
                value = value + two[half][peer, :, part].astype(jnp.float32)
            number = me * per_owner + half
            held = jnp.zeros((1, 1), jnp.int32)
            for adapter in range(counts.shape[0]):
                mine = jnp.full((1, 1), slots[adapter], jnp.int32) == number
                held = held + jnp.where(mine, counts[adapter], 0)
            out[half, :, part] = value * (adapter_factor / held.astype(jnp.float32))

    one_d, one_u = (one_d0, one_d1), (one_u0, one_u1)
    two_d, two_u = (two_d0, two_d1), (two_u0, two_u1)

    gather_first(0, gath_u)
    gather_own(1, adn, gath_d)
    gather_second(0, gath_u, True)
    gather_second(0, gath_u, False)
    gather_sibling(0, gath_u)
    loads[0].wait()
    loads[1].wait()
    share(0, z_up, partial_signal(og, gath_u))
    gather_first(1, gath_d)
    loads[2].wait()
    up_signal = shared(0, z_up)
    rows = gradient_rows(1 - core, up_signal)
    for piece in range(pieces[0]):
        sums_sibling(0, piece, rows, hid, sib_d, got_d)
    rows = gradient_rows(core, up_signal)
    sums_first(0, 0, rows, hid, got_d, sum_d, one_d)
    gather_second(1, gath_d, True)
    for piece in range(1, pieces[0]):
        sums_first(0, piece, rows, hid, got_d, sum_d, one_d)
    gather_second(1, gath_d, False)
    gather_sibling(1, gath_d)
    loads[3].wait()
    share(1, z_dn, partial_signal(hid, gath_d))

    all_rows = dp_count * per_owner * rank
    tokens_by_row = spread(up_signal, range(dp_count * per_owner)).T.astype(jnp.bfloat16)
    tile = tile_of(hid.shape[1])

    for at in range(hid.shape[1] // tile):
        cols = slice(at * tile, (at + 1) * tile)
        maps = gath_d[:, :, :, cols].reshape(all_rows, tile)
        term = jnp.dot(tokens_by_row, maps, preferred_element_type=jnp.float32)
        out_h[:, cols] = (adapter_factor * term).astype(out_h.dtype)

    down_signal = shared(1, z_dn)
    rows = gradient_rows(1 - core, down_signal)
    for piece in range(pieces[1]):
        sums_sibling(1, piece, rows, og, sib_u, got_u)
    sums_second(0, 0, sum_d, one_d, two_d)
    rows = gradient_rows(core, down_signal)
    for piece in range(pieces[1]):
        sums_first(1, piece, rows, og, got_u, sum_u, one_u)
    for piece in range(1, pieces[0]):
        sums_second(0, piece, sum_d, one_d, two_d)
    for piece in range(pieces[1]):
        sums_second(1, piece, sum_u, one_u, two_u)
    for piece in range(pieces[0]):
        sums_last(0, piece, sum_d, one_d, two_d, out_d)
    for piece in range(pieces[1]):
        sums_last(1, piece, sum_u, one_u, two_u, out_u)
    for copy in started:
        copy.wait_send()
    assert len(started) == sends, (len(started), sends)


def send_count(dp_count, tensor_count, per_owner, pieces):
    size_a, size_b = chip_grid(dp_count)
    total = 2 * (tensor_count - 1) + sum(pieces)
    for half in range(per_owner):
        n_first, n_second = (size_a, size_b) if half == 0 else (size_b, size_a)
        own = n_first + n_second - 1
        relayed = (n_first - 1) * n_second + (n_second - 1) * n_first
        back = (n_first - 1) * n_second + (n_second - 1)
        total += 2 * (own + relayed) + sum(pieces) * back
    return total


def on_device(output_gradient, hidden, adapter_down, adapter_up, counts, offsets, adapter_slot):
    dp_count, tensor_count = lax.axis_size("dp"), lax.axis_size("tensor")
    size_a, size_b = chip_grid(dp_count)
    chips = size_a * size_b
    per_owner, rank, wide = adapter_down.shape
    narrow = adapter_up.shape[2]
    tokens = hidden.shape[0]
    pieces = (2, 1)
    sends = send_count(dp_count, tensor_count, per_owner, pieces)
    bf16, f32 = jnp.bfloat16, jnp.float32
    dma = pltpu.SemaphoreType.DMA
    vmem = pl.BlockSpec(memory_space=pltpu.VMEM)
    any_space = pl.BlockSpec(memory_space=pl.ANY)
    scratch = [
        pltpu.SMEM(counts.shape, jnp.int32),
        pltpu.SMEM(offsets.shape, jnp.int32),
        pltpu.SMEM(adapter_slot.shape, jnp.int32),
        pltpu.VMEM((tokens, narrow), bf16),
        pltpu.VMEM((tokens, wide), bf16),
        pltpu.VMEM((dp_count, per_owner, rank, wide), bf16),
        pltpu.VMEM((dp_count, per_owner, rank, narrow), bf16),
        pltpu.VMEM((tensor_count, rank, tokens), f32),
        pltpu.VMEM((tensor_count, rank, tokens), f32),
    ]
    for _ in range(3):
        scratch.append(pltpu.VMEM((chips, per_owner, rank, wide), bf16))
        scratch.append(pltpu.VMEM((chips, per_owner, rank, narrow), bf16))
    for width in (wide, narrow):
        scratch.append(pltpu.VMEM((size_a, size_b, rank, width), bf16))
        scratch.append(pltpu.VMEM((size_b, size_a, rank, width), bf16))
    for width in (wide, narrow):
        scratch.append(pltpu.VMEM((size_b, rank, width), bf16))
        scratch.append(pltpu.VMEM((size_a, rank, width), bf16))
    scratch += [
        dma((7,)),
        dma((sends,)),
        dma((2, dp_count, per_owner)),
        dma((2, tensor_count)),
        dma((2, max(pieces))),
        dma((2, max(pieces), size_a, size_b)),
        dma((2, max(pieces), size_b, size_a)),
        dma((2, max(pieces), size_b)),
        dma((2, max(pieces), size_a)),
    ]
    rows = dp_count * per_owner * rank
    return pl.pallas_call(
        functools.partial(kernel, dp_count, tensor_count, sends, pieces),
        out_shape=(
            pltpu.VMEM((tokens, wide), bf16),
            pltpu.VMEM((per_owner, rank, wide), f32),
            pltpu.VMEM((per_owner, rank, narrow), f32),
        ),
        in_specs=[any_space] * 7,
        out_specs=(vmem, vmem, vmem),
        scratch_shapes=scratch,
        compiler_params=pltpu.CompilerParams(
            collective_id=0, has_side_effects=True, vmem_limit_bytes=48 * 2**20
        ),
        cost_estimate=pl.CostEstimate(
            flops=2 * rows * tokens * (3 * wide + 2 * narrow),
            bytes_accessed=2 * tokens * (2 * wide + narrow),
            transcendentals=0,
        ),
    )(*(
        pltpu.with_memory_space_constraint(array, pltpu.HBM)
        for array in (
            counts, offsets, adapter_slot, output_gradient, hidden, adapter_down, adapter_up
        )
    ))


def solution(mesh):
    placed = (
        P("dp", "tensor"),
        P("dp", "tensor"),
        P("dp", None, "tensor"),
        P("dp", None, "tensor"),
        P(),
        P(),
        P(),
    )
    return jax.shard_map(
        on_device,
        mesh=mesh,
        in_specs=placed,
        out_specs=(P("dp", "tensor"), P("dp", None, "tensor"), P("dp", None, "tensor")),
        check_vma=False,
    )
```

```python
import functools
import math

import jax
import jax.numpy as jnp
from jax import lax
from jax.experimental import pallas as pl
from jax.experimental.pallas import tpu as pltpu
from jax.sharding import PartitionSpec as P

adapter_factor = 2.0
MESH = pl.DeviceIdType.MESH


def chip_grid(dp_count):
    chips = dp_count // 2
    second = max(d for d in range(1, math.isqrt(chips) + 1) if chips % d == 0)
    return chips // second, second


def kernel(
    dp_count, tensor_count, sends, pieces,
    counts_in, offsets_in, slots_in, og_in, hid_in, adn, aup,
    out_h, out_d, out_u,
    counts, offsets, slots, og, hid, gath_d, gath_u, z_up, z_dn,
    sib_d, sib_u, got_d, got_u, sum_d, sum_u,
    one_d0, one_d1, one_u0, one_u1, two_d0, two_d1, two_u0, two_u1,
    load_sem, send_sem, gath_sem, z_sem, sib_sem, one_sem0, one_sem1, two_sem0, two_sem1,
):
    size_a, size_b = chip_grid(dp_count)
    chips = size_a * size_b
    tokens = og.shape[0]
    per_owner, rank = adn.shape[0], adn.shape[1]
    me = lax.axis_index("dp")
    me_t = lax.axis_index("tensor")
    core = me % 2
    chip = me // 2
    at_a, at_b = chip // size_b, chip % size_b
    sibling = chip * 2 + (1 - core)

    def chip_of(half, first, second):
        return first * size_b + second if half == 0 else second * size_b + first

    def axes(half):
        if half == 0:
            return at_a, size_a, at_b, size_b
        return at_b, size_b, at_a, size_a

    started = []

    def push(src, dst, recv, **device):
        copy = pltpu.make_async_remote_copy(
            src_ref=src, dst_ref=dst, send_sem=send_sem.at[len(started)], recv_sem=recv,
            device_id=device, device_id_type=MESH,
        )
        copy.start()
        started.append(copy)

    def arrived(dst, recv):
        pltpu.make_async_remote_copy(
            src_ref=dst, dst_ref=dst, send_sem=send_sem.at[0], recv_sem=recv,
            device_id={"dp": sibling}, device_id_type=MESH,
        ).wait_recv()

    loads = [
        pltpu.make_async_copy(aup, gath_u.at[me], load_sem.at[0]),
        pltpu.make_async_copy(og_in, og, load_sem.at[1]),
        pltpu.make_async_copy(hid_in, hid, load_sem.at[2]),
        pltpu.make_async_copy(adn, gath_d.at[me], load_sem.at[3]),
        pltpu.make_async_copy(counts_in, counts, load_sem.at[4]),
        pltpu.make_async_copy(offsets_in, offsets, load_sem.at[5]),
        pltpu.make_async_copy(slots_in, slots, load_sem.at[6]),
    ]
    for load in loads:
        load.start()

    barrier = pltpu.get_barrier_semaphore()
    partners = [{"dp": sibling}]
    for off in range(1, size_a):
        partners.append({"dp": (((at_a + off) % size_a) * size_b + at_b) * 2 + core})
    for off in range(1, size_b):
        partners.append({"dp": (at_a * size_b + (at_b + off) % size_b) * 2 + core})
    for off in range(1, tensor_count):
        partners.append({"tensor": (me_t + off) % tensor_count})
    for partner in partners:
        pl.semaphore_signal(barrier, inc=1, device_id=partner, device_id_type=MESH)
    pl.semaphore_wait(barrier, len(partners))

    def gather_own(which, own, gath, along_first):
        for half in range(per_owner):
            first, n_first, second, n_second = axes(half)
            for off in range(1, n_first if along_first else n_second):
                if along_first:
                    to = chip_of(half, (first + off) % n_first, second) * 2 + core
                else:
                    to = chip_of(half, first, (second + off) % n_second) * 2 + core
                push(
                    own.at[half], gath.at[me, half], gath_sem.at[which, me, half], dp=to
                )

    def gather_near(which, own, gath):
        for half in range(per_owner):
            push(own.at[half], gath.at[me, half], gath_sem.at[which, me, half], dp=sibling)

    def gather_first(which, gath):
        for half in range(per_owner):
            first, n_first, second, n_second = axes(half)
            for off in range(1, n_first):
                origin = chip_of(half, (first + off) % n_first, second) * 2 + core
                block, recv = gath.at[origin, half], gath_sem.at[which, origin, half]
                arrived(block, recv)
                for off2 in range(1, n_second):
                    to = chip_of(half, first, (second + off2) % n_second) * 2 + core
                    push(block, block, recv, dp=to)
                push(block, block, recv, dp=sibling)

    def gather_second(which, gath, near):
        for half in range(per_owner):
            first, n_first, second, n_second = axes(half)
            for off2 in range(1, n_second):
                for off in range(0, 1) if near else range(1, n_first):
                    origin = chip_of(
                        half, (first + off) % n_first, (second + off2) % n_second
                    ) * 2 + core
                    block, recv = gath.at[origin, half], gath_sem.at[which, origin, half]
                    arrived(block, recv)
                    push(block, block, recv, dp=sibling)

    def gather_sibling(which, gath):
        for other in range(chips):
            for half in range(per_owner):
                origin = other * 2 + (1 - core)
                arrived(gath.at[origin, half], gath_sem.at[which, origin, half])

    gather_own(0, aup, gath_u, True)
    gather_own(0, aup, gath_u, False)
    gather_near(0, aup, gath_u)
    gather_own(1, adn, gath_d, True)
    for load in loads[4:]:
        load.wait()
    position = me * tokens + lax.broadcasted_iota(jnp.int32, (1, tokens), 1)
    slot_of = jnp.zeros((1, tokens), jnp.int32)
    for adapter in range(counts.shape[0]):
        low = offsets[adapter]
        inside = (position >= low) & (position < low + counts[adapter])
        slot_of = slot_of + jnp.where(inside, slots[adapter], 0)

    def tile_of(width):
        return math.gcd(width, 1024)

    def partial_signal(values, gath):
        rows = dp_count * per_owner * rank
        scores = lax.dot_general(
            gath[...].reshape(rows, values.shape[1]), values[...], (((1,), (1,)), ((), ())),
            preferred_element_type=jnp.float32,
        ).reshape(dp_count * per_owner, rank, tokens)
        total = jnp.zeros((rank, tokens), jnp.float32)
        for slot in range(dp_count * per_owner):
            total = total + jnp.where(slot_of == slot, scores[slot], 0.0)
        return total

    def share(which, buffer, value):
        buffer[pl.ds(me_t, 1)] = value[None]
        for off in range(1, tensor_count):
            push(
                buffer.at[me_t], buffer.at[me_t], z_sem.at[which, me_t],
                tensor=(me_t + off) % tensor_count,
            )

    def shared(which, buffer):
        for off in range(1, tensor_count):
            origin = (me_t + off) % tensor_count
            arrived(buffer.at[origin], z_sem.at[which, origin])
        total = buffer[0]
        for origin in range(1, tensor_count):
            total = total + buffer[origin]
        return total.astype(jnp.bfloat16).astype(jnp.float32)

    def spread(signal, numbers):
        return jnp.concatenate(
            [jnp.where(slot_of == number, signal, 0.0) for number in numbers], axis=0
        )

    def numbers_of(which_core):
        return [
            (other * 2 + which_core) * per_owner + half
            for other in range(chips)
            for half in range(per_owner)
        ]

    def piece_of(which, piece, width):
        return pl.ds(piece * (width // pieces[which]), width // pieces[which])

    def gradient_rows(which_core, signal):
        return spread(signal, numbers_of(which_core)).astype(jnp.bfloat16)

    def tiles(which, piece, width):
        size = width // pieces[which]
        tile = math.gcd(size, 1024)
        return [pl.ds(piece * size + at, tile) for at in range(0, size, tile)]

    def sums_sibling(which, piece, rows, values, sib, got):
        for cols in tiles(which, piece, values.shape[1]):
            term = jnp.dot(rows, values[:, cols], preferred_element_type=jnp.float32)
            sib[:, :, :, cols] = term.astype(jnp.bfloat16).reshape(
                chips, per_owner, rank, cols.size
            )
        part = piece_of(which, piece, values.shape[1])
        push(
            sib.at[:, :, :, part], got.at[:, :, :, part], sib_sem.at[which, piece], dp=sibling
        )

    def sums_first(which, piece, rows, values, got, total, one):
        part = piece_of(which, piece, values.shape[1])
        arrived(got.at[:, :, :, part], sib_sem.at[which, piece])
        for cols in tiles(which, piece, values.shape[1]):
            term = jnp.dot(rows, values[:, cols], preferred_element_type=jnp.float32)
            term = term.reshape(chips, per_owner, rank, cols.size)
            term = term + got[:, :, :, cols].astype(jnp.float32)
            total[:, :, :, cols] = term.astype(jnp.bfloat16)
        sems = (one_sem0, one_sem1)
        for far in (True, False):
            for half in range(per_owner):
                first, n_first, second, n_second = axes(half)
                for off in range(1, n_first):
                    peer = (first + off) % n_first
                    to = chip_of(half, peer, second) * 2 + core
                    for off2 in range(1, n_second) if far else range(0, 1):
                        owner_second = (second + off2) % n_second
                        push(
                            total.at[chip_of(half, peer, owner_second), half, :, part],
                            one[half].at[first, owner_second, :, part],
                            sems[half].at[which, piece, first, owner_second],
                            dp=to,
                        )

    def sums_second(which, piece, total, one, two):
        part = piece_of(which, piece, total.shape[3])
        sems, sems2 = (one_sem0, one_sem1), (two_sem0, two_sem1)
        for half in range(per_owner):
            first, n_first, second, n_second = axes(half)
            for off2 in range(1, n_second):
                owner_second = (second + off2) % n_second
                owner = chip_of(half, first, owner_second)
                value = total[owner, half, :, part].astype(jnp.float32)
                for off in range(1, n_first):
                    peer = (first + off) % n_first
                    arrived(
                        one[half].at[peer, owner_second, :, part],
                        sems[half].at[which, piece, peer, owner_second],
                    )
                    value = value + one[half][peer, owner_second, :, part].astype(jnp.float32)
                total[pl.ds(owner, 1), half, :, part] = value.astype(jnp.bfloat16)[None]
                push(
                    total.at[owner, half, :, part], two[half].at[second, :, part],
                    sems2[half].at[which, piece, second], dp=owner * 2 + core,
                )

    def sums_last(which, piece, total, one, two, out):
        part = piece_of(which, piece, total.shape[3])
        sems, sems2 = (one_sem0, one_sem1), (two_sem0, two_sem1)
        for half in range(per_owner):
            first, n_first, second, n_second = axes(half)
            value = total[chip, half, :, part].astype(jnp.float32)
            for off in range(1, n_first):
                peer = (first + off) % n_first
                arrived(
                    one[half].at[peer, second, :, part],
                    sems[half].at[which, piece, peer, second],
                )
                value = value + one[half][peer, second, :, part].astype(jnp.float32)
            for off2 in range(1, n_second):
                peer = (second + off2) % n_second
                arrived(two[half].at[peer, :, part], sems2[half].at[which, piece, peer])
                value = value + two[half][peer, :, part].astype(jnp.float32)
            number = me * per_owner + half
            held = jnp.zeros((1, 1), jnp.int32)
            for adapter in range(counts.shape[0]):
                mine = jnp.full((1, 1), slots[adapter], jnp.int32) == number
                held = held + jnp.where(mine, counts[adapter], 0)
            out[half, :, part] = value * (adapter_factor / held.astype(jnp.float32))

    one_d, one_u = (one_d0, one_d1), (one_u0, one_u1)
    two_d, two_u = (two_d0, two_d1), (two_u0, two_u1)

    gather_first(0, gath_u)
    gather_own(1, adn, gath_d, False)
    gather_near(1, adn, gath_d)
    gather_second(0, gath_u, True)
    gather_second(0, gath_u, False)
    gather_sibling(0, gath_u)
    loads[0].wait()
    loads[1].wait()
    share(0, z_up, partial_signal(og, gath_u))
    gather_first(1, gath_d)
    loads[2].wait()
    up_signal = shared(0, z_up)
    rows = gradient_rows(1 - core, up_signal)
    for piece in range(pieces[0]):
        sums_sibling(0, piece, rows, hid, sib_d, got_d)
    rows = gradient_rows(core, up_signal)
    sums_first(0, 0, rows, hid, got_d, sum_d, one_d)
    gather_second(1, gath_d, True)
    for piece in range(1, pieces[0]):
        sums_first(0, piece, rows, hid, got_d, sum_d, one_d)
    gather_second(1, gath_d, False)
    gather_sibling(1, gath_d)
    loads[3].wait()
    share(1, z_dn, partial_signal(hid, gath_d))

    all_rows = dp_count * per_owner * rank
    tokens_by_row = spread(up_signal, range(dp_count * per_owner)).T.astype(jnp.bfloat16)
    tile = tile_of(hid.shape[1])

    for at in range(hid.shape[1] // tile):
        cols = slice(at * tile, (at + 1) * tile)
        maps = gath_d[:, :, :, cols].reshape(all_rows, tile)
        term = jnp.dot(tokens_by_row, maps, preferred_element_type=jnp.float32)
        out_h[:, cols] = (adapter_factor * term).astype(out_h.dtype)

    down_signal = shared(1, z_dn)
    rows = gradient_rows(1 - core, down_signal)
    for piece in range(pieces[1]):
        sums_sibling(1, piece, rows, og, sib_u, got_u)
    sums_second(0, 0, sum_d, one_d, two_d)
    rows = gradient_rows(core, down_signal)
    for piece in range(pieces[1]):
        sums_first(1, piece, rows, og, got_u, sum_u, one_u)
    for piece in range(1, pieces[0]):
        sums_second(0, piece, sum_d, one_d, two_d)
    for piece in range(pieces[1]):
        sums_second(1, piece, sum_u, one_u, two_u)
    for piece in range(pieces[0]):
        sums_last(0, piece, sum_d, one_d, two_d, out_d)
    for piece in range(pieces[1]):
        sums_last(1, piece, sum_u, one_u, two_u, out_u)
    for copy in started:
        copy.wait_send()
    assert len(started) == sends, (len(started), sends)


def send_count(dp_count, tensor_count, per_owner, pieces):
    size_a, size_b = chip_grid(dp_count)
    total = 2 * (tensor_count - 1) + sum(pieces)
    for half in range(per_owner):
        n_first, n_second = (size_a, size_b) if half == 0 else (size_b, size_a)
        own = n_first + n_second - 1
        relayed = (n_first - 1) * n_second + (n_second - 1) * n_first
        back = (n_first - 1) * n_second + (n_second - 1)
        total += 2 * (own + relayed) + sum(pieces) * back
    return total


def on_device(output_gradient, hidden, adapter_down, adapter_up, counts, offsets, adapter_slot):
    dp_count, tensor_count = lax.axis_size("dp"), lax.axis_size("tensor")
    size_a, size_b = chip_grid(dp_count)
    chips = size_a * size_b
    per_owner, rank, wide = adapter_down.shape
    narrow = adapter_up.shape[2]
    tokens = hidden.shape[0]
    pieces = (2, 1)
    sends = send_count(dp_count, tensor_count, per_owner, pieces)
    bf16, f32 = jnp.bfloat16, jnp.float32
    dma = pltpu.SemaphoreType.DMA
    vmem = pl.BlockSpec(memory_space=pltpu.VMEM)
    any_space = pl.BlockSpec(memory_space=pl.ANY)
    scratch = [
        pltpu.SMEM(counts.shape, jnp.int32),
        pltpu.SMEM(offsets.shape, jnp.int32),
        pltpu.SMEM(adapter_slot.shape, jnp.int32),
        pltpu.VMEM((tokens, narrow), bf16),
        pltpu.VMEM((tokens, wide), bf16),
        pltpu.VMEM((dp_count, per_owner, rank, wide), bf16),
        pltpu.VMEM((dp_count, per_owner, rank, narrow), bf16),
        pltpu.VMEM((tensor_count, rank, tokens), f32),
        pltpu.VMEM((tensor_count, rank, tokens), f32),
    ]
    for _ in range(3):
        scratch.append(pltpu.VMEM((chips, per_owner, rank, wide), bf16))
        scratch.append(pltpu.VMEM((chips, per_owner, rank, narrow), bf16))
    for width in (wide, narrow):
        scratch.append(pltpu.VMEM((size_a, size_b, rank, width), bf16))
        scratch.append(pltpu.VMEM((size_b, size_a, rank, width), bf16))
    for width in (wide, narrow):
        scratch.append(pltpu.VMEM((size_b, rank, width), bf16))
        scratch.append(pltpu.VMEM((size_a, rank, width), bf16))
    scratch += [
        dma((7,)),
        dma((sends,)),
        dma((2, dp_count, per_owner)),
        dma((2, tensor_count)),
        dma((2, max(pieces))),
        dma((2, max(pieces), size_a, size_b)),
        dma((2, max(pieces), size_b, size_a)),
        dma((2, max(pieces), size_b)),
        dma((2, max(pieces), size_a)),
    ]
    rows = dp_count * per_owner * rank
    return pl.pallas_call(
        functools.partial(kernel, dp_count, tensor_count, sends, pieces),
        out_shape=(
            pltpu.VMEM((tokens, wide), bf16),
            pltpu.VMEM((per_owner, rank, wide), f32),
            pltpu.VMEM((per_owner, rank, narrow), f32),
        ),
        in_specs=[any_space] * 7,
        out_specs=(vmem, vmem, vmem),
        scratch_shapes=scratch,
        compiler_params=pltpu.CompilerParams(
            collective_id=0, has_side_effects=True, vmem_limit_bytes=48 * 2**20
        ),
        cost_estimate=pl.CostEstimate(
            flops=2 * rows * tokens * (3 * wide + 2 * narrow),
            bytes_accessed=2 * tokens * (2 * wide + narrow),
            transcendentals=0,
        ),
    )(*(
        pltpu.with_memory_space_constraint(array, pltpu.HBM)
        for array in (
            counts, offsets, adapter_slot, output_gradient, hidden, adapter_down, adapter_up
        )
    ))


def solution(mesh):
    placed = (
        P("dp", "tensor"),
        P("dp", "tensor"),
        P("dp", None, "tensor"),
        P("dp", None, "tensor"),
        P(),
        P(),
        P(),
    )
    return jax.shard_map(
        on_device,
        mesh=mesh,
        in_specs=placed,
        out_specs=(P("dp", "tensor"), P("dp", None, "tensor"), P("dp", None, "tensor")),
        check_vma=False,
    )
```

```python
import functools
import math

import jax
import jax.numpy as jnp
from jax import lax
from jax.experimental import pallas as pl
from jax.experimental.pallas import tpu as pltpu
from jax.sharding import PartitionSpec as P

adapter_factor = 2.0
MESH = pl.DeviceIdType.MESH


def chip_grid(dp_count):
    chips = dp_count // 2
    second = max(d for d in range(1, math.isqrt(chips) + 1) if chips % d == 0)
    return chips // second, second


def kernel(
    dp_count, tensor_count, sends, pieces,
    counts_in, offsets_in, slots_in, og_in, hid_in, adn, aup,
    out_h, out_d, out_u,
    counts, offsets, slots, og, hid, gath_d, gath_u, z_up, z_dn,
    sib_d, sib_u, got_d, got_u, sum_d, sum_u,
    one_d0, one_d1, one_u0, one_u1, two_d0, two_d1, two_u0, two_u1,
    load_sem, send_sem, gath_sem, z_sem, sib_sem, one_sem0, one_sem1, two_sem0, two_sem1,
):
    size_a, size_b = chip_grid(dp_count)
    chips = size_a * size_b
    tokens = og.shape[0]
    per_owner, rank = adn.shape[0], adn.shape[1]
    me = lax.axis_index("dp")
    me_t = lax.axis_index("tensor")
    core = me % 2
    chip = me // 2
    at_a, at_b = chip // size_b, chip % size_b
    sibling = chip * 2 + (1 - core)

    def chip_of(half, first, second):
        return first * size_b + second if half == 0 else second * size_b + first

    def axes(half):
        if half == 0:
            return at_a, size_a, at_b, size_b
        return at_b, size_b, at_a, size_a

    started = []

    def push(src, dst, recv, **device):
        copy = pltpu.make_async_remote_copy(
            src_ref=src, dst_ref=dst, send_sem=send_sem.at[len(started)], recv_sem=recv,
            device_id=device, device_id_type=MESH,
        )
        copy.start()
        started.append(copy)

    def arrived(dst, recv):
        pltpu.make_async_remote_copy(
            src_ref=dst, dst_ref=dst, send_sem=send_sem.at[0], recv_sem=recv,
            device_id={"dp": sibling}, device_id_type=MESH,
        ).wait_recv()

    loads = [
        pltpu.make_async_copy(aup, gath_u.at[me], load_sem.at[0]),
        pltpu.make_async_copy(og_in, og, load_sem.at[1]),
        pltpu.make_async_copy(hid_in, hid, load_sem.at[2]),
        pltpu.make_async_copy(adn, gath_d.at[me], load_sem.at[3]),
        pltpu.make_async_copy(counts_in, counts, load_sem.at[4]),
        pltpu.make_async_copy(offsets_in, offsets, load_sem.at[5]),
        pltpu.make_async_copy(slots_in, slots, load_sem.at[6]),
    ]
    for load in loads:
        load.start()

    barrier = pltpu.get_barrier_semaphore()
    partners = [{"dp": sibling}]
    for off in range(1, size_a):
        partners.append({"dp": (((at_a + off) % size_a) * size_b + at_b) * 2 + core})
    for off in range(1, size_b):
        partners.append({"dp": (at_a * size_b + (at_b + off) % size_b) * 2 + core})
    for off in range(1, tensor_count):
        partners.append({"tensor": (me_t + off) % tensor_count})
    for partner in partners:
        pl.semaphore_signal(barrier, inc=1, device_id=partner, device_id_type=MESH)
    pl.semaphore_wait(barrier, len(partners))

    def gather_own(which, own, gath):
        for along_first in (True, False):
            for half in range(per_owner):
                first, n_first, second, n_second = axes(half)
                recv = gath_sem.at[which, me, half]
                for off in range(1, n_first if along_first else n_second):
                    if along_first:
                        to = chip_of(half, (first + off) % n_first, second) * 2 + core
                    else:
                        to = chip_of(half, first, (second + off) % n_second) * 2 + core
                    push(own.at[half], gath.at[me, half], recv, dp=to)
        for half in range(per_owner):
            push(own.at[half], gath.at[me, half], gath_sem.at[which, me, half], dp=sibling)

    def gather_first(which, gath):
        for half in range(per_owner):
            first, n_first, second, n_second = axes(half)
            for off in range(1, n_first):
                origin = chip_of(half, (first + off) % n_first, second) * 2 + core
                block, recv = gath.at[origin, half], gath_sem.at[which, origin, half]
                arrived(block, recv)
                for off2 in range(1, n_second):
                    to = chip_of(half, first, (second + off2) % n_second) * 2 + core
                    push(block, block, recv, dp=to)
                push(block, block, recv, dp=sibling)

    def gather_second(which, gath, near):
        for half in range(per_owner):
            first, n_first, second, n_second = axes(half)
            for off2 in range(1, n_second):
                for off in range(0, 1) if near else range(1, n_first):
                    origin = chip_of(
                        half, (first + off) % n_first, (second + off2) % n_second
                    ) * 2 + core
                    block, recv = gath.at[origin, half], gath_sem.at[which, origin, half]
                    arrived(block, recv)
                    push(block, block, recv, dp=sibling)

    def gather_sibling(which, gath):
        for other in range(chips):
            for half in range(per_owner):
                origin = other * 2 + (1 - core)
                arrived(gath.at[origin, half], gath_sem.at[which, origin, half])

    gather_own(0, aup, gath_u)
    for load in loads[4:]:
        load.wait()
    position = me * tokens + lax.broadcasted_iota(jnp.int32, (1, tokens), 1)
    slot_of = jnp.zeros((1, tokens), jnp.int32)
    for adapter in range(counts.shape[0]):
        low = offsets[adapter]
        inside = (position >= low) & (position < low + counts[adapter])
        slot_of = slot_of + jnp.where(inside, slots[adapter], 0)

    def tile_of(width):
        return math.gcd(width, 1024)

    def partial_signal(values, gath):
        rows = dp_count * per_owner * rank
        scores = lax.dot_general(
            gath[...].reshape(rows, values.shape[1]), values[...], (((1,), (1,)), ((), ())),
            preferred_element_type=jnp.float32,
        ).reshape(dp_count * per_owner, rank, tokens)
        total = jnp.zeros((rank, tokens), jnp.float32)
        for slot in range(dp_count * per_owner):
            total = total + jnp.where(slot_of == slot, scores[slot], 0.0)
        return total

    def share(which, buffer, value):
        buffer[pl.ds(me_t, 1)] = value[None]
        for off in range(1, tensor_count):
            push(
                buffer.at[me_t], buffer.at[me_t], z_sem.at[which, me_t],
                tensor=(me_t + off) % tensor_count,
            )

    def shared(which, buffer):
        for off in range(1, tensor_count):
            origin = (me_t + off) % tensor_count
            arrived(buffer.at[origin], z_sem.at[which, origin])
        total = buffer[0]
        for origin in range(1, tensor_count):
            total = total + buffer[origin]
        return total.astype(jnp.bfloat16).astype(jnp.float32)

    def spread(signal, numbers):
        return jnp.concatenate(
            [jnp.where(slot_of == number, signal, 0.0) for number in numbers], axis=0
        )

    def numbers_of(which_core):
        return [
            (other * 2 + which_core) * per_owner + half
            for other in range(chips)
            for half in range(per_owner)
        ]

    def piece_of(which, piece, width):
        return pl.ds(piece * (width // pieces[which]), width // pieces[which])

    def gradient_rows(which_core, signal):
        return spread(signal, numbers_of(which_core)).astype(jnp.bfloat16)

    def tiles(which, piece, width):
        size = width // pieces[which]
        tile = math.gcd(size, 1024)
        return [pl.ds(piece * size + at, tile) for at in range(0, size, tile)]

    def sums_sibling(which, piece, rows, values, sib, got):
        for cols in tiles(which, piece, values.shape[1]):
            term = jnp.dot(rows, values[:, cols], preferred_element_type=jnp.float32)
            sib[:, :, :, cols] = term.astype(jnp.bfloat16).reshape(
                chips, per_owner, rank, cols.size
            )
        part = piece_of(which, piece, values.shape[1])
        push(
            sib.at[:, :, :, part], got.at[:, :, :, part], sib_sem.at[which, piece], dp=sibling
        )

    def sums_first(which, piece, rows, values, got, total, one):
        part = piece_of(which, piece, values.shape[1])
        arrived(got.at[:, :, :, part], sib_sem.at[which, piece])
        for cols in tiles(which, piece, values.shape[1]):
            term = jnp.dot(rows, values[:, cols], preferred_element_type=jnp.float32)
            term = term.reshape(chips, per_owner, rank, cols.size)
            term = term + got[:, :, :, cols].astype(jnp.float32)
            total[:, :, :, cols] = term.astype(jnp.bfloat16)
        sems = (one_sem0, one_sem1)
        for far in (True, False):
            for half in range(per_owner):
                first, n_first, second, n_second = axes(half)
                for off in range(1, n_first):
                    peer = (first + off) % n_first
                    to = chip_of(half, peer, second) * 2 + core
                    for off2 in range(1, n_second) if far else range(0, 1):
                        owner_second = (second + off2) % n_second
                        push(
                            total.at[chip_of(half, peer, owner_second), half, :, part],
                            one[half].at[first, owner_second, :, part],
                            sems[half].at[which, piece, first, owner_second],
                            dp=to,
                        )

    def sums_second(which, piece, total, one, two):
        part = piece_of(which, piece, total.shape[3])
        sems, sems2 = (one_sem0, one_sem1), (two_sem0, two_sem1)
        for half in range(per_owner):
            first, n_first, second, n_second = axes(half)
            for off2 in range(1, n_second):
                owner_second = (second + off2) % n_second
                owner = chip_of(half, first, owner_second)
                value = total[owner, half, :, part].astype(jnp.float32)
                for off in range(1, n_first):
                    peer = (first + off) % n_first
                    arrived(
                        one[half].at[peer, owner_second, :, part],
                        sems[half].at[which, piece, peer, owner_second],
                    )
                    value = value + one[half][peer, owner_second, :, part].astype(jnp.float32)
                total[pl.ds(owner, 1), half, :, part] = value.astype(jnp.bfloat16)[None]
                push(
                    total.at[owner, half, :, part], two[half].at[second, :, part],
                    sems2[half].at[which, piece, second], dp=owner * 2 + core,
                )

    def sums_last(which, piece, total, one, two, out):
        part = piece_of(which, piece, total.shape[3])
        sems, sems2 = (one_sem0, one_sem1), (two_sem0, two_sem1)
        for half in range(per_owner):
            first, n_first, second, n_second = axes(half)
            value = total[chip, half, :, part].astype(jnp.float32)
            for off in range(1, n_first):
                peer = (first + off) % n_first
                arrived(
                    one[half].at[peer, second, :, part],
                    sems[half].at[which, piece, peer, second],
                )
                value = value + one[half][peer, second, :, part].astype(jnp.float32)
            for off2 in range(1, n_second):
                peer = (second + off2) % n_second
                arrived(two[half].at[peer, :, part], sems2[half].at[which, piece, peer])
                value = value + two[half][peer, :, part].astype(jnp.float32)
            number = me * per_owner + half
            held = jnp.zeros((1, 1), jnp.int32)
            for adapter in range(counts.shape[0]):
                mine = jnp.full((1, 1), slots[adapter], jnp.int32) == number
                held = held + jnp.where(mine, counts[adapter], 0)
            out[half, :, part] = value * (adapter_factor / held.astype(jnp.float32))

    one_d, one_u = (one_d0, one_d1), (one_u0, one_u1)
    two_d, two_u = (two_d0, two_d1), (two_u0, two_u1)

    gather_first(0, gath_u)
    gather_own(1, adn, gath_d)
    gather_second(0, gath_u, True)
    gather_second(0, gath_u, False)
    gather_sibling(0, gath_u)
    loads[0].wait()
    loads[1].wait()
    share(0, z_up, partial_signal(og, gath_u))
    gather_first(1, gath_d)
    loads[2].wait()
    up_signal = shared(0, z_up)
    rows = gradient_rows(1 - core, up_signal)
    for piece in range(pieces[0]):
        sums_sibling(0, piece, rows, hid, sib_d, got_d)
    rows = gradient_rows(core, up_signal)
    sums_first(0, 0, rows, hid, got_d, sum_d, one_d)
    gather_second(1, gath_d, True)
    for piece in range(1, pieces[0]):
        sums_first(0, piece, rows, hid, got_d, sum_d, one_d)
    gather_second(1, gath_d, False)
    gather_sibling(1, gath_d)
    loads[3].wait()
    share(1, z_dn, partial_signal(hid, gath_d))

    all_rows = dp_count * per_owner * rank
    tokens_by_row = spread(up_signal, range(dp_count * per_owner)).T.astype(jnp.bfloat16)
    tile = tile_of(hid.shape[1])

    for at in range(hid.shape[1] // tile):
        cols = slice(at * tile, (at + 1) * tile)
        maps = gath_d[:, :, :, cols].reshape(all_rows, tile)
        term = jnp.dot(tokens_by_row, maps, preferred_element_type=jnp.float32)
        out_h[:, cols] = (adapter_factor * term).astype(out_h.dtype)

    down_signal = shared(1, z_dn)
    rows = gradient_rows(1 - core, down_signal)
    for piece in range(pieces[1]):
        sums_sibling(1, piece, rows, og, sib_u, got_u)
    sums_second(0, 0, sum_d, one_d, two_d)
    rows = gradient_rows(core, down_signal)
    for piece in range(pieces[1]):
        sums_first(1, piece, rows, og, got_u, sum_u, one_u)
    for piece in range(1, pieces[0]):
        sums_second(0, piece, sum_d, one_d, two_d)
    for piece in range(pieces[1]):
        sums_second(1, piece, sum_u, one_u, two_u)
    for piece in range(pieces[0]):
        sums_last(0, piece, sum_d, one_d, two_d, out_d)
    for piece in range(pieces[1]):
        sums_last(1, piece, sum_u, one_u, two_u, out_u)
    for copy in started:
        copy.wait_send()
    assert len(started) == sends, (len(started), sends)


def write_out(h, d, u, out_h, out_d, out_u, sem):
    copies = [
        pltpu.make_async_copy(src, dst, sem.at[at])
        for at, (src, dst) in enumerate(((h, out_h), (d, out_d), (u, out_u)))
    ]
    for copy in copies:
        copy.start()
    for copy in copies:
        copy.wait()


def send_count(dp_count, tensor_count, per_owner, pieces):
    size_a, size_b = chip_grid(dp_count)
    total = 2 * (tensor_count - 1) + sum(pieces)
    for half in range(per_owner):
        n_first, n_second = (size_a, size_b) if half == 0 else (size_b, size_a)
        own = n_first + n_second - 1
        relayed = (n_first - 1) * n_second + (n_second - 1) * n_first
        back = (n_first - 1) * n_second + (n_second - 1)
        total += 2 * (own + relayed) + sum(pieces) * back
    return total


def on_device(output_gradient, hidden, adapter_down, adapter_up, counts, offsets, adapter_slot):
    dp_count, tensor_count = lax.axis_size("dp"), lax.axis_size("tensor")
    size_a, size_b = chip_grid(dp_count)
    chips = size_a * size_b
    per_owner, rank, wide = adapter_down.shape
    narrow = adapter_up.shape[2]
    tokens = hidden.shape[0]
    pieces = (2, 1)
    sends = send_count(dp_count, tensor_count, per_owner, pieces)
    bf16, f32 = jnp.bfloat16, jnp.float32
    dma = pltpu.SemaphoreType.DMA
    vmem = pl.BlockSpec(memory_space=pltpu.VMEM)
    any_space = pl.BlockSpec(memory_space=pl.ANY)
    scratch = [
        pltpu.SMEM(counts.shape, jnp.int32),
        pltpu.SMEM(offsets.shape, jnp.int32),
        pltpu.SMEM(adapter_slot.shape, jnp.int32),
        pltpu.VMEM((tokens, narrow), bf16),
        pltpu.VMEM((tokens, wide), bf16),
        pltpu.VMEM((dp_count, per_owner, rank, wide), bf16),
        pltpu.VMEM((dp_count, per_owner, rank, narrow), bf16),
        pltpu.VMEM((tensor_count, rank, tokens), f32),
        pltpu.VMEM((tensor_count, rank, tokens), f32),
    ]
    for _ in range(3):
        scratch.append(pltpu.VMEM((chips, per_owner, rank, wide), bf16))
        scratch.append(pltpu.VMEM((chips, per_owner, rank, narrow), bf16))
    for width in (wide, narrow):
        scratch.append(pltpu.VMEM((size_a, size_b, rank, width), bf16))
        scratch.append(pltpu.VMEM((size_b, size_a, rank, width), bf16))
    for width in (wide, narrow):
        scratch.append(pltpu.VMEM((size_b, rank, width), bf16))
        scratch.append(pltpu.VMEM((size_a, rank, width), bf16))
    scratch += [
        dma((7,)),
        dma((sends,)),
        dma((2, dp_count, per_owner)),
        dma((2, tensor_count)),
        dma((2, max(pieces))),
        dma((2, max(pieces), size_a, size_b)),
        dma((2, max(pieces), size_b, size_a)),
        dma((2, max(pieces), size_b)),
        dma((2, max(pieces), size_a)),
    ]
    rows = dp_count * per_owner * rank
    results = pl.pallas_call(
        functools.partial(kernel, dp_count, tensor_count, sends, pieces),
        out_shape=(
            pltpu.VMEM((tokens, wide), bf16),
            pltpu.VMEM((per_owner, rank, wide), f32),
            pltpu.VMEM((per_owner, rank, narrow), f32),
        ),
        in_specs=[any_space] * 7,
        out_specs=(vmem, vmem, vmem),
        scratch_shapes=scratch,
        compiler_params=pltpu.CompilerParams(
            collective_id=0, has_side_effects=True, vmem_limit_bytes=48 * 2**20
        ),
        cost_estimate=pl.CostEstimate(
            flops=2 * rows * tokens * (3 * wide + 2 * narrow),
            bytes_accessed=2 * tokens * (2 * wide + narrow),
            transcendentals=0,
        ),
    )(*(
        pltpu.with_memory_space_constraint(array, pltpu.HBM)
        for array in (
            counts, offsets, adapter_slot, output_gradient, hidden, adapter_down, adapter_up
        )
    ))
    return pl.pallas_call(
        write_out,
        out_shape=tuple(pltpu.HBM(r.shape, r.dtype) for r in results),
        in_specs=[any_space] * 3,
        out_specs=(any_space,) * 3,
        scratch_shapes=[dma((3,))],
        compiler_params=pltpu.CompilerParams(vmem_limit_bytes=2 * 2**20),
        cost_estimate=pl.CostEstimate(
            flops=0, bytes_accessed=2 * tokens * wide, transcendentals=0
        ),
    )(*(pltpu.with_memory_space_constraint(r, pltpu.VMEM) for r in results))


def solution(mesh):
    placed = (
        P("dp", "tensor"),
        P("dp", "tensor"),
        P("dp", None, "tensor"),
        P("dp", None, "tensor"),
        P(),
        P(),
        P(),
    )
    return jax.shard_map(
        on_device,
        mesh=mesh,
        in_specs=placed,
        out_specs=(P("dp", "tensor"), P("dp", None, "tensor"), P("dp", None, "tensor")),
        check_vma=False,
    )
```

```python
import functools
import math

import jax
import jax.numpy as jnp
from jax import lax
from jax.experimental import pallas as pl
from jax.experimental.pallas import tpu as pltpu
from jax.sharding import PartitionSpec as P

adapter_factor = 2.0
MESH = pl.DeviceIdType.MESH


def chip_grid(dp_count):
    chips = dp_count // 2
    second = max(d for d in range(1, math.isqrt(chips) + 1) if chips % d == 0)
    return chips // second, second


def kernel(
    dp_count, tensor_count, sends, pieces,
    counts_in, offsets_in, slots_in, og_in, hid_in, adn, aup,
    out_h, out_d, out_u,
    counts, offsets, slots, og, hid, gath_d, gath_u, z_up, z_dn,
    sib_d, sib_u, got_d, got_u, sum_d, sum_u,
    one_d0, one_d1, one_u0, one_u1, two_d0, two_d1, two_u0, two_u1,
    load_sem, send_sem, gath_sem, z_sem, sib_sem, one_sem0, one_sem1, two_sem0, two_sem1,
):
    size_a, size_b = chip_grid(dp_count)
    chips = size_a * size_b
    tokens = og.shape[0]
    per_owner, rank = adn.shape[0], adn.shape[1]
    me = lax.axis_index("dp")
    me_t = lax.axis_index("tensor")
    core = me % 2
    chip = me // 2
    at_a, at_b = chip // size_b, chip % size_b
    sibling = chip * 2 + (1 - core)

    def chip_of(half, first, second):
        return first * size_b + second if half == 0 else second * size_b + first

    def axes(half):
        if half == 0:
            return at_a, size_a, at_b, size_b
        return at_b, size_b, at_a, size_a

    started = []

    def push(src, dst, recv, **device):
        copy = pltpu.make_async_remote_copy(
            src_ref=src, dst_ref=dst, send_sem=send_sem.at[len(started)], recv_sem=recv,
            device_id=device, device_id_type=MESH,
        )
        copy.start()
        started.append(copy)

    def arrived(dst, recv):
        pltpu.make_async_remote_copy(
            src_ref=dst, dst_ref=dst, send_sem=send_sem.at[0], recv_sem=recv,
            device_id={"dp": sibling}, device_id_type=MESH,
        ).wait_recv()

    loads = [
        pltpu.make_async_copy(aup, gath_u.at[me], load_sem.at[0]),
        pltpu.make_async_copy(og_in, og, load_sem.at[1]),
        pltpu.make_async_copy(hid_in, hid, load_sem.at[2]),
        pltpu.make_async_copy(adn, gath_d.at[me], load_sem.at[3]),
        pltpu.make_async_copy(counts_in, counts, load_sem.at[4]),
        pltpu.make_async_copy(offsets_in, offsets, load_sem.at[5]),
        pltpu.make_async_copy(slots_in, slots, load_sem.at[6]),
    ]
    for load in loads:
        load.start()

    barrier = pltpu.get_barrier_semaphore()
    partners = [{"dp": sibling}]
    for off in range(1, size_a):
        partners.append({"dp": (((at_a + off) % size_a) * size_b + at_b) * 2 + core})
    for off in range(1, size_b):
        partners.append({"dp": (at_a * size_b + (at_b + off) % size_b) * 2 + core})
    for off in range(1, tensor_count):
        partners.append({"tensor": (me_t + off) % tensor_count})
    for partner in partners:
        pl.semaphore_signal(barrier, inc=1, device_id=partner, device_id_type=MESH)
    pl.semaphore_wait(barrier, len(partners))

    def gather_own(which, own, gath):
        for along_first in (True, False):
            for half in range(per_owner):
                first, n_first, second, n_second = axes(half)
                recv = gath_sem.at[which, me, half]
                for off in range(1, n_first if along_first else n_second):
                    if along_first:
                        to = chip_of(half, (first + off) % n_first, second) * 2 + core
                    else:
                        to = chip_of(half, first, (second + off) % n_second) * 2 + core
                    push(own.at[half], gath.at[me, half], recv, dp=to)
        for half in range(per_owner):
            push(own.at[half], gath.at[me, half], gath_sem.at[which, me, half], dp=sibling)

    def gather_first(which, gath):
        for half in range(per_owner):
            first, n_first, second, n_second = axes(half)
            for off in range(1, n_first):
                origin = chip_of(half, (first + off) % n_first, second) * 2 + core
                block, recv = gath.at[origin, half], gath_sem.at[which, origin, half]
                arrived(block, recv)
                for off2 in range(1, n_second):
                    to = chip_of(half, first, (second + off2) % n_second) * 2 + core
                    push(block, block, recv, dp=to)
                push(block, block, recv, dp=sibling)

    def gather_second(which, gath, near):
        for half in range(per_owner):
            first, n_first, second, n_second = axes(half)
            for off2 in range(1, n_second):
                for off in range(0, 1) if near else range(1, n_first):
                    origin = chip_of(
                        half, (first + off) % n_first, (second + off2) % n_second
                    ) * 2 + core
                    block, recv = gath.at[origin, half], gath_sem.at[which, origin, half]
                    arrived(block, recv)
                    push(block, block, recv, dp=sibling)

    def gather_sibling(which, gath):
        for other in range(chips):
            for half in range(per_owner):
                origin = other * 2 + (1 - core)
                arrived(gath.at[origin, half], gath_sem.at[which, origin, half])

    gather_own(0, aup, gath_u)
    for load in loads[4:]:
        load.wait()
    position = me * tokens + lax.broadcasted_iota(jnp.int32, (1, tokens), 1)
    slot_of = jnp.zeros((1, tokens), jnp.int32)
    for adapter in range(counts.shape[0]):
        low = offsets[adapter]
        inside = (position >= low) & (position < low + counts[adapter])
        slot_of = slot_of + jnp.where(inside, slots[adapter], 0)

    def tile_of(width):
        return math.gcd(width, 1024)

    def partial_signal(values, gath):
        rows = dp_count * per_owner * rank
        scores = lax.dot_general(
            gath[...].reshape(rows, values.shape[1]), values[...], (((1,), (1,)), ((), ())),
            preferred_element_type=jnp.float32,
        ).reshape(dp_count * per_owner, rank, tokens)
        total = jnp.zeros((rank, tokens), jnp.float32)
        for slot in range(dp_count * per_owner):
            total = total + jnp.where(slot_of == slot, scores[slot], 0.0)
        return total

    def share(which, buffer, value):
        buffer[pl.ds(me_t, 1)] = value[None]
        for off in range(1, tensor_count):
            push(
                buffer.at[me_t], buffer.at[me_t], z_sem.at[which, me_t],
                tensor=(me_t + off) % tensor_count,
            )

    def shared(which, buffer):
        for off in range(1, tensor_count):
            origin = (me_t + off) % tensor_count
            arrived(buffer.at[origin], z_sem.at[which, origin])
        total = buffer[0]
        for origin in range(1, tensor_count):
            total = total + buffer[origin]
        return total.astype(jnp.bfloat16).astype(jnp.float32)

    def spread(signal, numbers):
        return jnp.concatenate(
            [jnp.where(slot_of == number, signal, 0.0) for number in numbers], axis=0
        )

    def numbers_of(which_core):
        return [
            (other * 2 + which_core) * per_owner + half
            for other in range(chips)
            for half in range(per_owner)
        ]

    def piece_of(which, piece, width):
        return pl.ds(piece * (width // pieces[which]), width // pieces[which])

    def gradient_rows(which_core, signal):
        return spread(signal, numbers_of(which_core)).astype(jnp.bfloat16)

    def tiles(which, piece, width):
        size = width // pieces[which]
        tile = math.gcd(size, 1024)
        return [pl.ds(piece * size + at, tile) for at in range(0, size, tile)]

    def sums_sibling(which, piece, rows, values, sib, got):
        for cols in tiles(which, piece, values.shape[1]):
            term = jnp.dot(rows, values[:, cols], preferred_element_type=jnp.float32)
            sib[:, :, :, cols] = term.astype(jnp.bfloat16).reshape(
                chips, per_owner, rank, cols.size
            )
        part = piece_of(which, piece, values.shape[1])
        push(
            sib.at[:, :, :, part], got.at[:, :, :, part], sib_sem.at[which, piece], dp=sibling
        )

    def sums_first(which, piece, rows, values, got, total, one):
        part = piece_of(which, piece, values.shape[1])
        arrived(got.at[:, :, :, part], sib_sem.at[which, piece])
        for cols in tiles(which, piece, values.shape[1]):
            term = jnp.dot(rows, values[:, cols], preferred_element_type=jnp.float32)
            term = term.reshape(chips, per_owner, rank, cols.size)
            term = term + got[:, :, :, cols].astype(jnp.float32)
            total[:, :, :, cols] = term.astype(jnp.bfloat16)
        sems = (one_sem0, one_sem1)
        for far in (True, False):
            for half in range(per_owner):
                first, n_first, second, n_second = axes(half)
                for off in range(1, n_first):
                    peer = (first + off) % n_first
                    to = chip_of(half, peer, second) * 2 + core
                    for off2 in range(1, n_second) if far else range(0, 1):
                        owner_second = (second + off2) % n_second
                        push(
                            total.at[chip_of(half, peer, owner_second), half, :, part],
                            one[half].at[first, owner_second, :, part],
                            sems[half].at[which, piece, first, owner_second],
                            dp=to,
                        )

    def sums_second(which, piece, total, one, two):
        part = piece_of(which, piece, total.shape[3])
        sems, sems2 = (one_sem0, one_sem1), (two_sem0, two_sem1)
        for half in range(per_owner):
            first, n_first, second, n_second = axes(half)
            for off2 in range(1, n_second):
                owner_second = (second + off2) % n_second
                owner = chip_of(half, first, owner_second)
                value = total[owner, half, :, part].astype(jnp.float32)
                for off in range(1, n_first):
                    peer = (first + off) % n_first
                    arrived(
                        one[half].at[peer, owner_second, :, part],
                        sems[half].at[which, piece, peer, owner_second],
                    )
                    value = value + one[half][peer, owner_second, :, part].astype(jnp.float32)
                total[pl.ds(owner, 1), half, :, part] = value.astype(jnp.bfloat16)[None]
                push(
                    total.at[owner, half, :, part], two[half].at[second, :, part],
                    sems2[half].at[which, piece, second], dp=owner * 2 + core,
                )

    def sums_last(which, piece, total, one, two, out):
        part = piece_of(which, piece, total.shape[3])
        sems, sems2 = (one_sem0, one_sem1), (two_sem0, two_sem1)
        for half in range(per_owner):
            first, n_first, second, n_second = axes(half)
            value = total[chip, half, :, part].astype(jnp.float32)
            for off in range(1, n_first):
                peer = (first + off) % n_first
                arrived(
                    one[half].at[peer, second, :, part],
                    sems[half].at[which, piece, peer, second],
                )
                value = value + one[half][peer, second, :, part].astype(jnp.float32)
            for off2 in range(1, n_second):
                peer = (second + off2) % n_second
                arrived(two[half].at[peer, :, part], sems2[half].at[which, piece, peer])
                value = value + two[half][peer, :, part].astype(jnp.float32)
            number = me * per_owner + half
            held = jnp.zeros((1, 1), jnp.int32)
            for adapter in range(counts.shape[0]):
                mine = jnp.full((1, 1), slots[adapter], jnp.int32) == number
                held = held + jnp.where(mine, counts[adapter], 0)
            out[half, :, part] = value * (adapter_factor / held.astype(jnp.float32))

    one_d, one_u = (one_d0, one_d1), (one_u0, one_u1)
    two_d, two_u = (two_d0, two_d1), (two_u0, two_u1)

    gather_first(0, gath_u)
    gather_own(1, adn, gath_d)
    gather_second(0, gath_u, True)
    gather_second(0, gath_u, False)
    gather_sibling(0, gath_u)
    loads[0].wait()
    loads[1].wait()
    share(0, z_up, partial_signal(og, gath_u))
    gather_first(1, gath_d)
    loads[2].wait()
    up_signal = shared(0, z_up)
    rows = gradient_rows(1 - core, up_signal)
    for piece in range(pieces[0]):
        sums_sibling(0, piece, rows, hid, sib_d, got_d)
    rows = gradient_rows(core, up_signal)
    sums_first(0, 0, rows, hid, got_d, sum_d, one_d)
    gather_second(1, gath_d, True)
    for piece in range(1, pieces[0]):
        sums_first(0, piece, rows, hid, got_d, sum_d, one_d)
    gather_second(1, gath_d, False)
    gather_sibling(1, gath_d)
    loads[3].wait()
    share(1, z_dn, partial_signal(hid, gath_d))

    all_rows = dp_count * per_owner * rank
    tokens_by_row = spread(up_signal, range(dp_count * per_owner)).T.astype(jnp.bfloat16)
    tile = tile_of(hid.shape[1])
    steps = hid.shape[1] // tile

    def hidden_tiles(begin, end):
        for at in range(begin, end):
            cols = slice(at * tile, (at + 1) * tile)
            maps = gath_d[:, :, :, cols].reshape(all_rows, tile)
            term = jnp.dot(tokens_by_row, maps, preferred_element_type=jnp.float32)
            out_h[:, cols] = (adapter_factor * term).astype(out_h.dtype)

    hidden_tiles(0, steps // 2)
    down_signal = shared(1, z_dn)
    rows = gradient_rows(1 - core, down_signal)
    for piece in range(pieces[1]):
        sums_sibling(1, piece, rows, og, sib_u, got_u)
    hidden_tiles(steps // 2, steps)
    sums_second(0, 0, sum_d, one_d, two_d)
    rows = gradient_rows(core, down_signal)
    for piece in range(pieces[1]):
        sums_first(1, piece, rows, og, got_u, sum_u, one_u)
    for piece in range(1, pieces[0]):
        sums_second(0, piece, sum_d, one_d, two_d)
    for piece in range(pieces[1]):
        sums_second(1, piece, sum_u, one_u, two_u)
    for piece in range(pieces[0]):
        sums_last(0, piece, sum_d, one_d, two_d, out_d)
    for piece in range(pieces[1]):
        sums_last(1, piece, sum_u, one_u, two_u, out_u)
    for copy in started:
        copy.wait_send()
    assert len(started) == sends, (len(started), sends)


def write_out(h, d, u, out_h, out_d, out_u, sem):
    copies = [
        pltpu.make_async_copy(src, dst, sem.at[at])
        for at, (src, dst) in enumerate(((h, out_h), (d, out_d), (u, out_u)))
    ]
    for copy in copies:
        copy.start()
    for copy in copies:
        copy.wait()


def send_count(dp_count, tensor_count, per_owner, pieces):
    size_a, size_b = chip_grid(dp_count)
    total = 2 * (tensor_count - 1) + sum(pieces)
    for half in range(per_owner):
        n_first, n_second = (size_a, size_b) if half == 0 else (size_b, size_a)
        own = n_first + n_second - 1
        relayed = (n_first - 1) * n_second + (n_second - 1) * n_first
        back = (n_first - 1) * n_second + (n_second - 1)
        total += 2 * (own + relayed) + sum(pieces) * back
    return total


def on_device(output_gradient, hidden, adapter_down, adapter_up, counts, offsets, adapter_slot):
    dp_count, tensor_count = lax.axis_size("dp"), lax.axis_size("tensor")
    size_a, size_b = chip_grid(dp_count)
    chips = size_a * size_b
    per_owner, rank, wide = adapter_down.shape
    narrow = adapter_up.shape[2]
    tokens = hidden.shape[0]
    pieces = (2, 1)
    sends = send_count(dp_count, tensor_count, per_owner, pieces)
    bf16, f32 = jnp.bfloat16, jnp.float32
    dma = pltpu.SemaphoreType.DMA
    vmem = pl.BlockSpec(memory_space=pltpu.VMEM)
    any_space = pl.BlockSpec(memory_space=pl.ANY)
    scratch = [
        pltpu.SMEM(counts.shape, jnp.int32),
        pltpu.SMEM(offsets.shape, jnp.int32),
        pltpu.SMEM(adapter_slot.shape, jnp.int32),
        pltpu.VMEM((tokens, narrow), bf16),
        pltpu.VMEM((tokens, wide), bf16),
        pltpu.VMEM((dp_count, per_owner, rank, wide), bf16),
        pltpu.VMEM((dp_count, per_owner, rank, narrow), bf16),
        pltpu.VMEM((tensor_count, rank, tokens), f32),
        pltpu.VMEM((tensor_count, rank, tokens), f32),
    ]
    for _ in range(3):
        scratch.append(pltpu.VMEM((chips, per_owner, rank, wide), bf16))
        scratch.append(pltpu.VMEM((chips, per_owner, rank, narrow), bf16))
    for width in (wide, narrow):
        scratch.append(pltpu.VMEM((size_a, size_b, rank, width), bf16))
        scratch.append(pltpu.VMEM((size_b, size_a, rank, width), bf16))
    for width in (wide, narrow):
        scratch.append(pltpu.VMEM((size_b, rank, width), bf16))
        scratch.append(pltpu.VMEM((size_a, rank, width), bf16))
    scratch += [
        dma((7,)),
        dma((sends,)),
        dma((2, dp_count, per_owner)),
        dma((2, tensor_count)),
        dma((2, max(pieces))),
        dma((2, max(pieces), size_a, size_b)),
        dma((2, max(pieces), size_b, size_a)),
        dma((2, max(pieces), size_b)),
        dma((2, max(pieces), size_a)),
    ]
    rows = dp_count * per_owner * rank
    results = pl.pallas_call(
        functools.partial(kernel, dp_count, tensor_count, sends, pieces),
        out_shape=(
            pltpu.VMEM((tokens, wide), bf16),
            pltpu.VMEM((per_owner, rank, wide), f32),
            pltpu.VMEM((per_owner, rank, narrow), f32),
        ),
        in_specs=[any_space] * 7,
        out_specs=(vmem, vmem, vmem),
        scratch_shapes=scratch,
        compiler_params=pltpu.CompilerParams(
            collective_id=0, has_side_effects=True, vmem_limit_bytes=48 * 2**20
        ),
        cost_estimate=pl.CostEstimate(
            flops=2 * rows * tokens * (3 * wide + 2 * narrow),
            bytes_accessed=2 * tokens * (2 * wide + narrow),
            transcendentals=0,
        ),
    )(*(
        pltpu.with_memory_space_constraint(array, pltpu.HBM)
        for array in (
            counts, offsets, adapter_slot, output_gradient, hidden, adapter_down, adapter_up
        )
    ))
    return pl.pallas_call(
        write_out,
        out_shape=tuple(pltpu.HBM(r.shape, r.dtype) for r in results),
        in_specs=[any_space] * 3,
        out_specs=(any_space,) * 3,
        scratch_shapes=[dma((3,))],
        compiler_params=pltpu.CompilerParams(vmem_limit_bytes=2 * 2**20),
        cost_estimate=pl.CostEstimate(
            flops=0, bytes_accessed=2 * tokens * wide, transcendentals=0
        ),
    )(*(pltpu.with_memory_space_constraint(r, pltpu.VMEM) for r in results))


def solution(mesh):
    placed = (
        P("dp", "tensor"),
        P("dp", "tensor"),
        P("dp", None, "tensor"),
        P("dp", None, "tensor"),
        P(),
        P(),
        P(),
    )
    return jax.shard_map(
        on_device,
        mesh=mesh,
        in_specs=placed,
        out_specs=(P("dp", "tensor"), P("dp", None, "tensor"), P("dp", None, "tensor")),
        check_vma=False,
    )
```
